256 devices in a mesh: seq: 32 (over x, y, core), head: 8 (over z).
Axes of the slice: x: 4, y: 4, z: 8, core: 2. Of those that a mesh axis runs over, the one named last changes fastest.
Arguments:
- video_feat: bfloat16 [128, 16, 64, 512], P('seq', 'head'), may hold values from -6 to 6
- clip_frames: int32 [64], replicated, may hold values from 1 to 3, as said below
- clip_offset: int32 [64], replicated, may hold values from 0 to 127, as said below
- conv_weight: bfloat16 [3, 3, 3, 512, 512], P(None, None, None, None, 'head'), may hold values from -0.0546875 to 0.0546875
- conv_bias: float32 [512], replicated, may hold values from -3 to 3
- latent_weight: bfloat16 [512, 16], replicated, may hold values from -0.25 to 0.25
- latent_bias: float32 [16], replicated, may hold values from -6 to 6
- embed_weight: bfloat16 [64, 3072], replicated, may hold values from -0.75 to 0.75
- embed_bias: float32 [3072], replicated, may hold values from -3 to 3
- modulation: bfloat16 [64, 6144], replicated, may hold values from -3 to 3
- qkv_weight: bfloat16 [3072, 6144], P(None, 'head'), may hold values from -1 to 1
- qkv_bias: float32 [6144], P('head'), may hold values from -3 to 3
- q_gain: float32 [128], replicated, may hold values from 0.5 to 5
- k_gain: float32 [128], replicated, may hold values from 0.5 to 5
Outputs:
- attn_out: bfloat16 [32768, 2048], P('seq', 'head')
The draws below stay inside these ranges and needn't reach their ends.
Inputs may be any that keep to these rules, and one draw needn't show every extreme that they name: `clip_frames`: laid end to end in order the clips fill the 128 source frames exactly; every shard's 4 destination slots hold exactly two clips. Clip i takes the destination slots clip_offset[i] to clip_offset[i] + clip_frames[i] - 1, all inside one shard's slots q * 4 to (q + 1) * 4 - 1; the clips' slots cover all 128 slots once.
All inputs are finite; a program needn't handle non-finite values.
Results may differ from the reference program's by a relative error of at most 0.008.
Values may be sent and summed in bfloat16 or wider, within the bound.
No kernel may reach another device: no remote copies, remote signals or barrier semaphores. Data moves between devices by JAX's collectives and lax.ppermute only.
A program may use at most 192 MiB of HBM per device.

```python
import math
import jax
import jax.numpy as jnp
from jax import lax

D = 3072
HD = 128
HEADS = 16
C = 512
LAT = 16
F_DEV = 4
PC = 32
NF = 128
NR = 16
NW = 64
PF = 64
NCLIP = 64
GROUP = 1024
TOKENS = 32768
N_SEQ = 32
N_HEAD = 8


def clip_layout(key):
    shards = NCLIP // 2
    leading = jax.random.randint(jax.random.fold_in(key, 101), (shards,), 1, F_DEV).astype(jnp.int32)
    leading = leading.at[0].set(1)
    leading = leading.at[shards - 1].set(F_DEV - 1)
    lengths = jnp.stack([leading, F_DEV - leading], axis=1).reshape(-1)
    bases = jnp.arange(shards, dtype=jnp.int32) * F_DEV
    offsets = jnp.stack([bases, bases + leading], axis=1).reshape(-1)
    order = jax.random.permutation(jax.random.fold_in(key, 102), NCLIP)
    return (lengths[order].astype(jnp.int32), offsets[order].astype(jnp.int32))


def draw_clip_frames(key, part):
    shared = clip_layout(key)
    return shared[0]


def draw_clip_offset(key, part):
    shared = clip_layout(key)
    return shared[1]


def draw_qkv_weight(key, part):
    key = jax.random.fold_in(key, 5)
    base = jax.random.normal(key, (D, HEADS, 3, HD), jnp.float32) * D ** (-0.5)
    return base.reshape(D, 3 * HEADS * HD).astype(jnp.bfloat16)


def draw_q_gain(key, part):
    key = jax.random.fold_in(key, 7)
    return jax.random.uniform(key, (HD,), jnp.float32, 0.5, 2.0)


def draw_k_gain(key, part):
    key = jax.random.fold_in(key, 8)
    return jax.random.uniform(key, (HD,), jnp.float32, 0.5, 2.0)


def level_of(stream_key, shape, cuts, low, top_value):
    def one(axis_at, parts):
        heights = jax.random.uniform(jax.random.fold_in(jax.random.fold_in(stream_key, 6), axis_at), (parts,), jnp.float32, low / len(cuts), top_value / len(cuts))
        return jnp.repeat(jnp.exp(heights), shape[axis_at] // parts).reshape((-1,) + (1,) * (len(shape) - axis_at - 1))

    level = one(*cuts[0])
    for cut in cuts[1:]:
        level = level * one(*cut)
    return level


def bell_draw(rng, shape, deviation, limit, pieces=(), held_as=jnp.bfloat16):
    entries = jax.random.normal(rng, shape, jnp.float32) * deviation
    if len(pieces) > 0:
        entries = level_of(rng, shape, pieces, -0.22, 0.18) * entries
    return jnp.clip(entries, min=-limit, max=limit).astype(held_as)


def setup_inputs(seed: int = 0) -> dict:
    streams_of = jax.random.split(jax.random.key(seed), 15)
    return {
        "video_feat": bell_draw(streams_of[0], (NF, NR, NW, C), 1.0, 6.0, ((0, 32), (1, 8))),
        "clip_frames": draw_clip_frames(jax.random.fold_in(streams_of[14], 71), 0),
        "clip_offset": draw_clip_offset(jax.random.fold_in(streams_of[14], 71), 0),
        "conv_weight": bell_draw(streams_of[3], (3, 3, 3, C, C), (27 * C) ** -0.5, 0.0546875, ((4, 8),)),
        "conv_bias": bell_draw(streams_of[4], (C,), 0.5, 3.0, (), jnp.float32),
        "latent_weight": bell_draw(streams_of[5], (C, LAT), C ** -0.5, 0.25),
        "latent_bias": bell_draw(streams_of[6], (LAT,), 1.0, 6.0, (), jnp.float32),
        "embed_weight": bell_draw(streams_of[7], (PF, D), PF ** -0.5, 0.75),
        "embed_bias": bell_draw(streams_of[8], (D,), 0.5, 3.0, (), jnp.float32),
        "modulation": bell_draw(streams_of[9], (NCLIP, 2 * D), 0.5, 3.0),
        "qkv_weight": draw_qkv_weight(jax.random.fold_in(streams_of[14], 71), 0),
        "qkv_bias": bell_draw(streams_of[11], (3 * HEADS * HD,), 0.5, 3.0, ((0, 8),), jnp.float32),
        "q_gain": draw_q_gain(jax.random.fold_in(streams_of[14], 71), 0),
        "k_gain": draw_k_gain(jax.random.fold_in(streams_of[14], 71), 0),
    }


latent_scale = 0.476986
norm_eps = 1e-06

def frame_tables(clip_frames, clip_offset, count):
    ends = jnp.cumsum(clip_frames).astype(jnp.int32)
    starts = (ends - clip_frames).astype(jnp.int32)
    frame_ids = jnp.arange(count, dtype=jnp.int32)
    member = (frame_ids[:, None] >= starts[None, :]) & (frame_ids[:, None] < ends[None, :])
    first = lax.optimization_barrier(jnp.sum(jnp.where(member, starts[None, :], 0), axis=1)).astype(jnp.int32)
    target = (lax.optimization_barrier(jnp.sum(jnp.where(member, clip_offset[None, :], 0), axis=1)) + frame_ids - first).astype(jnp.int32)
    return (first, target)

def slot_tables(clip_frames, clip_offset, modulation, shard, frames):
    slots = (shard * frames + jnp.arange(frames, dtype=jnp.int32)).astype(jnp.int32)
    member = (slots[:, None] >= clip_offset[None, :]) & (slots[:, None] < (clip_offset + clip_frames)[None, :])
    numbers = jnp.arange(clip_frames.shape[0], dtype=jnp.int32)
    clip_ids = lax.optimization_barrier(jnp.sum(jnp.where(member, numbers[None, :], 0), axis=1)).astype(jnp.int32)
    slot_mod = jnp.dot(member.astype(jnp.bfloat16), modulation, preferred_element_type=jnp.float32)
    return (clip_ids, slot_mod)

def modulate(tokens, frames, columns, slot_mod, embed_weight, embed_bias):
    width = embed_weight.shape[1]
    embedded = jnp.dot(tokens, embed_weight, preferred_element_type=jnp.float32) + embed_bias
    mean = lax.optimization_barrier(jnp.mean(embedded, axis=-1, keepdims=True))
    centered = embedded - mean
    variance = lax.optimization_barrier(jnp.mean(centered * centered, axis=-1, keepdims=True))
    normed = (centered * lax.rsqrt(variance + norm_eps)).reshape(-1, frames, columns, width)
    shift = slot_mod[None, :, None, :width]
    scale = slot_mod[None, :, None, width:]
    return (normed * (1.0 + scale) + shift).reshape(-1, width).astype(jnp.bfloat16)

def rms_scale(part, gain):
    factor = lax.rsqrt(lax.optimization_barrier(jnp.mean(part * part, axis=-1, keepdims=True)) + norm_eps)
    return (part * factor * gain).astype(jnp.bfloat16)

def attend(qkv, head_size, row_clip, q_gain, k_gain):
    rows = qkv.shape[0]
    split = qkv.reshape(rows, -1, 3, head_size)
    query = rms_scale(split[:, :, 0], q_gain).astype(jnp.float32)
    keys = rms_scale(split[:, :, 1], k_gain).astype(jnp.float32)
    values = split[:, :, 2].astype(jnp.bfloat16).astype(jnp.float32)
    scores = jnp.einsum('qhd,khd->hqk', query, keys) / math.sqrt(head_size)
    same = row_clip[:, None] == row_clip[None, :]
    scores = jnp.where(same[None], scores, -jnp.inf)
    top = lax.optimization_barrier(jnp.max(scores, axis=-1, keepdims=True))
    expo = jnp.exp(scores - top)
    weights = (expo / lax.optimization_barrier(jnp.sum(expo, axis=-1, keepdims=True))).astype(jnp.bfloat16).astype(jnp.float32)
    output = jnp.einsum('hqk,khd->qhd', weights, values)
    return output.astype(jnp.bfloat16).reshape(rows, -1)

def reference(video_feat, clip_frames, clip_offset, conv_weight, conv_bias, latent_weight, latent_bias, embed_weight, embed_bias, modulation, qkv_weight, qkv_bias, q_gain, k_gain):
    frames_all = video_feat.shape[0]
    height = video_feat.shape[1]
    width = video_feat.shape[2]
    channels = video_feat.shape[3]
    first, target = frame_tables(clip_frames, clip_offset, frames_all)
    act = jax.nn.silu(video_feat.astype(jnp.float32)).astype(jnp.bfloat16)
    padded = jnp.pad(act, ((0, 0), (1, 1), (1, 1), (0, 0)))
    frame_ids = jnp.arange(frames_all, dtype=jnp.int32)
    conv = jnp.zeros((frames_all * height * width, channels), jnp.float32)
    for delay in range(3):
        source = jnp.maximum(frame_ids - (2 - delay), first).astype(jnp.int32)
        picked = jnp.take(padded, source, axis=0)
        for row_step in range(3):
            for col_step in range(3):
                window = picked[:, row_step:row_step + height, col_step:col_step + width, :].reshape(-1, channels)
                conv = conv + jnp.dot(window, conv_weight[delay, row_step, col_step], preferred_element_type=jnp.float32)
    section = (video_feat.astype(jnp.float32).reshape(-1, channels) + conv + conv_bias).astype(jnp.bfloat16)
    latent = ((jnp.dot(section, latent_weight, preferred_element_type=jnp.float32) + latent_bias) * latent_scale).astype(jnp.bfloat16)
    lat_count = latent_weight.shape[1]
    patch = latent.reshape(frames_all, N_HEAD, 2, PC, 2, lat_count).transpose(0, 1, 3, 5, 2, 4)
    patch = patch.reshape(frames_all, N_HEAD, PC, 4 * lat_count)
    inverse = jnp.argsort(target).astype(jnp.int32)
    placed = jnp.take(patch, inverse, axis=0)
    grouped = placed.reshape(N_SEQ, F_DEV, N_HEAD, PC, 4 * lat_count).transpose(0, 2, 1, 3, 4)
    grouped = grouped.reshape(N_SEQ, GROUP, 4 * lat_count)
    row_slots = (jnp.arange(GROUP, dtype=jnp.int32) // PC % F_DEV).astype(jnp.int32)

    def shard_attention(inputs):
        tokens, shard = inputs
        clip_ids, slot_mod = slot_tables(clip_frames, clip_offset, modulation, shard, F_DEV)
        hidden = modulate(tokens, F_DEV, PC, slot_mod, embed_weight, embed_bias)
        qkv = jnp.dot(hidden, qkv_weight, preferred_element_type=jnp.float32) + qkv_bias
        return attend(qkv, HD, jnp.take(clip_ids, row_slots), q_gain, k_gain)
    result = lax.map(shard_attention, (grouped, jnp.arange(N_SEQ, dtype=jnp.int32)))
    return result.reshape(TOKENS, HEADS * HD)
```

```python
import functools
import math

import jax
import jax.numpy as jnp
from jax import lax
from jax.experimental import pallas as pl
from jax.experimental.pallas import tpu as pltpu
from jax.sharding import PartitionSpec as P

latent_scale = 0.476986
norm_eps = 1e-06
f32 = jnp.float32
bf16 = jnp.bfloat16
MIB = 1024 * 1024
NT = (((1,), (1,)), ((), ()))


def dot(a, b, dims=(((1,), (0,)), ((), ()))):
    return lax.dot_general(a, b, dims, preferred_element_type=f32)


def split2(value):
    high = value.astype(bf16)
    return high, (value - high.astype(f32)).astype(bf16)


def iota(shape, dim):
    return lax.broadcasted_iota(jnp.int32, shape, dim)


def fold_kernel(place_ref, weight_ref, latent_ref, out_ref):
    out_ref[...] = dot(latent_ref[...], weight_ref[0], (((0,), (0,)), ((), ())))


def fold_tap(weight, latent_weight, tap, band):
    taps, outs, ins = weight.shape
    lats = latent_weight.shape[1]
    return pl.pallas_call(
        fold_kernel,
        grid_spec=pltpu.PrefetchScalarGridSpec(
            num_scalar_prefetch=1,
            grid=(1,),
            in_specs=[
                pl.BlockSpec((1, outs, ins), lambda i, place: (place[0], 0, 0)),
                pl.BlockSpec((outs, lats), lambda i, place: (place[1], 0)),
            ],
            out_specs=pl.BlockSpec((lats, ins), lambda i, place: (0, 0)),
        ),
        out_shape=jax.ShapeDtypeStruct((lats, ins), f32),
        cost_estimate=pl.CostEstimate(flops=10**6, bytes_accessed=150000, transcendentals=0),
        name="fold_tap",
    )(jnp.stack([tap, band]).astype(jnp.int32), weight, latent_weight)


def prep_kernel(main, prev, lowm, highm, lowp, highp, lat, cbias, lbias, act, base):
    def silu(value):
        value = value.astype(f32)
        half = 0.5 * value
        return (half * jnp.tanh(half) + half).astype(bf16)

    for frame in range(6):
        if frame < 2:
            rows = (lowp[frame], prev[frame, 0], prev[frame, 1], highp[frame])
        else:
            own = frame - 2
            rows = (lowm[own], main[own, 0], main[own, 1], highm[own])
        for row, value in enumerate(rows):
            at = (frame * 4 + row) * 64
            act[at : at + 64, :] = silu(value)
    weight = lat[...]
    const = jnp.sum(weight.astype(f32) * cbias[...], axis=1, keepdims=True) + lbias[...]
    for frame in range(4):
        own = main[frame].reshape(128, 512)
        base[:, frame * 128 : frame * 128 + 128] = dot(weight, own, NT) + const


def prepare(video, prev, lowm, highm, lowp, highp, lat, conv_bias, latent_bias):
    return pl.pallas_call(
        prep_kernel,
        out_shape=(
            jax.ShapeDtypeStruct((1536, 512), bf16),
            jax.ShapeDtypeStruct((16, 512), f32),
        ),
        compiler_params=pltpu.CompilerParams(vmem_limit_bytes=24 * MIB),
        cost_estimate=pl.CostEstimate(flops=2 * 10**7, bytes_accessed=3 * 10**6, transcendentals=800000),
        name="prepare",
    )(video, prev, lowm, highm, lowp, highp, lat, conv_bias.reshape(1, -1), latent_bias.reshape(-1, 1))


def conv_kernel(source, target, act, folded, base, out, taps):
    weight = folded[...]
    for frame in range(6):
        taps[frame] = dot(weight[:432], act[frame * 256 : frame * 256 + 256, :], NT)
    out[...] = jnp.zeros_like(out)
    lane = iota((16, 128), 1)
    column = lane % 64
    row = iota((128, 128), 0)
    pos = iota((128, 128), 1)
    own_half = (pos % 64) // 32 == row // 64
    own_cell = (pos // 64) * 2 + pos % 2 == row % 4
    keep = own_half & own_cell
    repeat = (iota((128, 16), 0) % 64 // 4 == iota((128, 16), 1)).astype(bf16)
    pick = ((lane % 32) // 2 == iota((16, 128), 0)).astype(bf16)
    for frame in range(4):
        total = None
        for delay in range(3):
            part = taps[source[frame * 3 + delay], delay * 144 : delay * 144 + 144, :]
            total = part if total is None else total + part
        sums = []
        for col in range(3):
            at = [total[(a * 3 + col) * 16 : (a * 3 + col) * 16 + 16] for a in range(3)]
            sums.append(at[0][:, 0:128] + at[1][:, 64:192] + at[2][:, 128:256])
        left = jnp.where(column == 0, 0.0, pltpu.roll(sums[0], 1, 1))
        right = jnp.where(column == 63, 0.0, pltpu.roll(sums[2], 127, 1))
        own = base[:, frame * 128 : frame * 128 + 128]
        latent = ((own + sums[1] + left + right) * latent_scale).astype(bf16)
        wide = jnp.where(keep, dot(repeat, latent), 0.0).astype(bf16)
        out[target[frame]] = dot(pick, wide, NT).astype(bf16)


def convolve(source, target, act, folded, base, slots):
    smem = pl.BlockSpec(memory_space=pltpu.SMEM)
    vmem = pl.BlockSpec(memory_space=pltpu.VMEM)
    return pl.pallas_call(
        conv_kernel,
        in_specs=[smem, smem, vmem, vmem, vmem],
        out_specs=vmem,
        out_shape=jax.ShapeDtypeStruct((slots, 16, 128), bf16),
        scratch_shapes=[pltpu.VMEM((6, 432, 256), f32)],
        compiler_params=pltpu.CompilerParams(vmem_limit_bytes=24 * MIB),
        cost_estimate=pl.CostEstimate(flops=7 * 10**8, bytes_accessed=3 * 10**6, transcendentals=0),
        name="convolve",
    )(source, target, act, folded, base)


def mix_kernel(
    member, modulation, embed, bias, qkv_w, qkv_b, mix, rows, gram, gvec, left
):
    step = pl.program_id(0)
    width = embed.shape[1]
    chunk = 512

    @pl.when(step == 0)
    def _():
        mean = jnp.sum(embed[...].astype(f32), axis=1, keepdims=True) / width
        bias_mean = jnp.sum(bias[...], axis=1, keepdims=True) / width
        whole = jnp.zeros((80, 80), f32)
        for at in range(0, width, chunk):
            here = slice(at, at + chunk)
            centred = embed[:, here].astype(f32) - mean
            cbias = bias[:, here] - bias_mean
            scale = 1.0 + dot(member[...], modulation[:, width + at : width + at + chunk])
            shift = dot(member[...], modulation[:, here])
            first, second = scale[0:1], scale[1:2]
            high, low = split2(centred * first)
            left[0:64, here] = high
            left[64:128, here] = low
            high, low = split2(centred * second)
            left[128:192, here] = high
            left[192:256, here] = low
            high, low = split2(jnp.concatenate([cbias * first, cbias * second], axis=0))
            left[256:272, here] = jnp.concatenate(
                [high.astype(f32), low.astype(f32), shift[0:2], jnp.zeros((10, chunk), f32)], axis=0
            ).astype(bf16)
            full = jnp.concatenate([centred, cbias, jnp.zeros((15, chunk), f32)], axis=0)
            high, low = split2(full)
            whole = whole + (dot(high, high, NT) + dot(high, low, NT) + dot(low, high, NT))
        whole = whole * (1.0 / width)
        square = whole[0:64, 0:64]
        blank = jnp.zeros((64, 64), f32)
        block = jnp.concatenate(
            [
                jnp.concatenate([square, blank], axis=1),
                jnp.concatenate([blank, square], axis=1),
            ],
            axis=0,
        )
        top = block.astype(bf16)
        rest = block - top.astype(f32)
        mid = rest.astype(bf16)
        gram[0] = top
        gram[1] = mid
        gram[2] = (rest - mid.astype(f32)).astype(bf16)
        cross = 2.0 * whole[64:65, 0:64]
        const = jnp.broadcast_to(whole[64:65, 64:65], (1, 128))
        gvec[...] = jnp.concatenate(
            [jnp.concatenate([cross, cross], axis=1), const, jnp.zeros((6, 128), f32)], axis=0
        )

    product = dot(left[...], qkv_w[...])
    cols = product.shape[1]
    empty = jnp.zeros((64, cols), bf16)
    for clip in range(2):
        at = clip * 128
        high, low = split2(product[at : at + 64] + product[at + 64 : at + 128])
        mix[clip, 0] = jnp.concatenate([high, empty, low, empty], axis=0)
        mix[clip, 1] = jnp.concatenate([empty, high, empty, low], axis=0)
    tail = product[256:272]
    rows[...] = jnp.concatenate(
        [tail[0:2] + tail[2:4], tail[4:6] + qkv_b[...], jnp.zeros((4, cols), f32)], axis=0
    )


def mix_weights(member, modulation, embed_weight, embed_bias, qkv_weight, qkv_bias):
    width = embed_weight.shape[1]
    cols = 256
    whole = lambda shape: pl.BlockSpec(shape, lambda n: (0,) * len(shape))
    return pl.pallas_call(
        mix_kernel,
        grid=(qkv_weight.shape[1] // cols,),
        in_specs=[
            whole((8, 64)),
            whole((64, 2 * width)),
            whole((64, width)),
            whole((1, width)),
            pl.BlockSpec((width, cols), lambda n: (0, n)),
            pl.BlockSpec((1, cols), lambda n: (0, n)),
        ],
        out_specs=[
            pl.BlockSpec((2, 2, 256, cols), lambda n: (0, 0, 0, n)),
            pl.BlockSpec((8, cols), lambda n: (0, n)),
            whole((3, 128, 128)),
            whole((8, 128)),
        ],
        out_shape=[
            jax.ShapeDtypeStruct((2, 2, 256, 768), bf16),
            jax.ShapeDtypeStruct((8, 768), f32),
            jax.ShapeDtypeStruct((3, 128, 128), bf16),
            jax.ShapeDtypeStruct((8, 128), f32),
        ],
        scratch_shapes=[pltpu.VMEM((272, width), bf16)],
        compiler_params=pltpu.CompilerParams(vmem_limit_bytes=24 * MIB),
        cost_estimate=pl.CostEstimate(flops=13 * 10**8, bytes_accessed=6 * 10**6, transcendentals=0),
        name="mix_weights",
    )(
        member, modulation, embed_weight, embed_bias.reshape(1, -1), qkv_weight, qkv_bias.reshape(1, -1)
    )


def attend_kernel(lead, tokens, mix, rows, gram, gvec, q_gain, k_gain, out, query, keys, values):
    factor = math.log2(math.e) / math.sqrt(128)
    gain_q = q_gain[...] * factor
    gain_k = k_gain[...]
    low_lane = iota((128, 128), 1) < 64
    for frame in range(4):
        later = frame >= lead[0]
        clip = later.astype(jnp.int32)
        slope = jnp.where(later, rows[1:2, :], rows[0:1, :])
        offset = jnp.where(later, rows[3:4, :], rows[2:3, :])
        own = tokens[:, frame].reshape(128, 128)
        twice = jnp.concatenate([own, own], axis=1)
        spread = dot(own, gram[0]) + dot(own, gram[1]) + dot(own, gram[2])
        terms = (spread + gvec[0:1, :]) * own.astype(f32)
        for half in range(2):
            mine = jnp.where(low_lane == (half == 0), terms, 0.0)
            variance = jnp.sum(mine, axis=1, keepdims=True) + gvec[1:2, 0:1]
            scale = lax.rsqrt(jnp.maximum(variance, 0.0) + norm_eps)
            qkv = scale * (dot(twice, mix[clip, half]) + slope) + offset
            at = frame * 256 + half * 128
            for head in range(2):
                part = qkv[:, head * 384 : head * 384 + 128]
                norm = lax.rsqrt(jnp.mean(part * part, axis=1, keepdims=True) + norm_eps)
                query[head, at : at + 128, :] = (part * norm * gain_q).astype(bf16)
                part = qkv[:, head * 384 + 128 : head * 384 + 256]
                norm = lax.rsqrt(jnp.mean(part * part, axis=1, keepdims=True) + norm_eps)
                keys[head, at : at + 128, :] = (part * norm * gain_k).astype(bf16)
                values[head, at : at + 128, :] = qkv[:, head * 384 + 256 : head * 384 + 384].astype(bf16)

    def group(begin, end):
        for head in range(2):
            key = keys[head, begin * 256 : end * 256, :]
            value = values[head, begin * 256 : end * 256, :]
            for frame in range(begin, end):
                score = dot(query[head, frame * 256 : frame * 256 + 256, :], key, NT)
                top = jnp.max(score, axis=1, keepdims=True)
                expo = jnp.exp2(score - top)
                total = jnp.sum(expo, axis=1, keepdims=True)
                result = (dot(expo.astype(bf16), value) / total).astype(bf16)
                for half in range(2):
                    out[:, frame, half, :, head * 128 : head * 128 + 128] = result[
                        half * 128 : half * 128 + 128
                    ].reshape(8, 16, 128)

    for first in (1, 2, 3):

        @pl.when(lead[0] == first)
        def _(first=first):
            group(0, first)
            group(first, 4)


def attend(lead, tokens, mix, rows, gram, gvec, q_gain, k_gain):
    smem = pl.BlockSpec(memory_space=pltpu.SMEM)
    vmem = pl.BlockSpec(memory_space=pltpu.VMEM)
    return pl.pallas_call(
        attend_kernel,
        in_specs=[smem] + [vmem] * 7,
        out_specs=vmem,
        out_shape=jax.ShapeDtypeStruct((8, 4, 2, 16, 256), bf16),
        scratch_shapes=[pltpu.VMEM((2, 1024, 128), bf16)] * 3,
        compiler_params=pltpu.CompilerParams(vmem_limit_bytes=32 * MIB),
        cost_estimate=pl.CostEstimate(flops=10**9, bytes_accessed=3 * 10**6, transcendentals=1300000),
        name="attend",
    )(lead, tokens, mix, rows, gram, gvec, q_gain.reshape(1, -1), k_gain.reshape(1, -1))


def shift_pairs(seqs, heads, seq_step, head_step):
    pairs = []
    for seq in range(seqs):
        for head in range(heads):
            to_seq, to_head = seq + seq_step, head + head_step
            if 0 <= to_seq < seqs and 0 <= to_head < heads:
                pairs.append((seq * heads + head, to_seq * heads + to_head))
    return pairs


def spread_all(value, axis):
    count = lax.axis_size(axis)
    return lax.all_to_all(jnp.broadcast_to(value[None], (count,) + value.shape), axis, 0, 0)


def per_device(
    video_feat,
    clip_frames,
    clip_offset,
    conv_weight,
    conv_bias,
    latent_weight,
    latent_bias,
    embed_weight,
    embed_bias,
    modulation,
    qkv_weight,
    qkv_bias,
    q_gain,
    k_gain,
):
    seqs, heads = lax.axis_size("seq"), lax.axis_size("head")
    seq, band = lax.axis_index("seq"), lax.axis_index("head")
    frames = video_feat.shape[0]
    send = lambda value, a, b: lax.ppermute(value, ("seq", "head"), shift_pairs(seqs, heads, a, b))

    weight = conv_weight.transpose(0, 1, 2, 4, 3).reshape(27, conv_weight.shape[4], -1)
    part = fold_tap(weight, latent_weight, jnp.minimum(seq, 26), band)
    tap = jnp.sum(spread_all(part, "head"), axis=0).astype(bf16)
    folded = spread_all(tap, "seq").reshape(seqs * 16, -1)

    prev = send(video_feat[2:], 1, 0)
    lowm = send(video_feat[:, 1], 0, 1)
    highm = send(video_feat[:, 0], 0, -1)
    lowp = send(video_feat[2:, 1], 1, 1)
    highp = send(video_feat[2:, 0], 1, -1)
    act, base = prepare(
        video_feat, prev, lowm, highm, lowp, highp, latent_weight.T, conv_bias, latent_bias
    )

    count = clip_frames.shape[0]
    numbers = jnp.arange(count, dtype=jnp.int32)
    starts = jnp.sum(jnp.where(numbers[None, :] < numbers[:, None], clip_frames[None, :], 0), axis=1)
    ids = seq * frames + jnp.arange(frames, dtype=jnp.int32)
    first = jnp.max(jnp.where(starts[None, :] <= ids[:, None], starts[None, :], 0), axis=1)
    offset = jnp.sum(jnp.where(starts[None, :] == first[:, None], clip_offset[None, :], 0), axis=1)
    target = jnp.clip(offset + ids - first, 0, seqs * frames - 1)
    delays = jnp.arange(3, dtype=jnp.int32)
    source = jnp.maximum(ids[:, None] - 2 + delays[None, :], first[:, None]) - seq * frames + 2
    source = jnp.clip(source, 0, frames + 1).reshape(-1)
    leading = clip_offset == seq * frames
    lead = jnp.sum(jnp.where(leading, clip_frames, 0)).reshape(1)
    trailing = (clip_offset > seq * frames) & (clip_offset < (seq + 1) * frames)
    member = jnp.concatenate(
        [leading[None], trailing[None], jnp.zeros((6, count), jnp.bool_)], axis=0
    ).astype(bf16)

    mix, rows, gram, gvec = mix_weights(
        member, modulation, embed_weight, embed_bias, qkv_weight, qkv_bias
    )

    placed = convolve(source, target, act, folded, base, seqs * frames)
    routed = lax.all_to_all(placed.reshape(seqs, frames, 16, 128), "seq", 0, 0)
    slots = jnp.sum(routed, axis=0)
    tokens = spread_all(slots, "head")
    out = attend(lead, tokens, mix, rows, gram, gvec, q_gain, k_gain)
    return out.reshape(heads * frames * 32, 256)


def solution(mesh):
    placed = (
        P("seq", "head", None, None),
        P(),
        P(),
        P(None, None, None, None, "head"),
        P(),
        P(),
        P(),
        P(),
        P(),
        P(),
        P(None, "head"),
        P("head"),
        P(),
        P(),
    )
    return jax.shard_map(
        per_device, mesh=mesh, in_specs=placed, out_specs=P("seq", "head"), check_vma=False
    )
```

```python
import functools
import math

import jax
import jax.numpy as jnp
from jax import lax
from jax.experimental import pallas as pl
from jax.experimental.pallas import tpu as pltpu
from jax.sharding import PartitionSpec as P

latent_scale = 0.476986
norm_eps = 1e-06
f32 = jnp.float32
bf16 = jnp.bfloat16
MIB = 1024 * 1024
NT = (((1,), (1,)), ((), ()))


def dot(a, b, dims=(((1,), (0,)), ((), ()))):
    return lax.dot_general(a, b, dims, preferred_element_type=f32)


def split2(value):
    high = value.astype(bf16)
    return high, (value - high.astype(f32)).astype(bf16)


def iota(shape, dim):
    return lax.broadcasted_iota(jnp.int32, shape, dim)


def fold_kernel(weight, latent, out, tap_buf, lat_buf, sems):
    band = lax.axis_index("head")
    last = weight.shape[0] - 1
    base = lax.axis_index("seq") // 2 * 2
    copies = [
        pltpu.make_async_copy(weight.at[jnp.minimum(base, last)], tap_buf.at[0], sems.at[0]),
        pltpu.make_async_copy(weight.at[jnp.minimum(base + 1, last)], tap_buf.at[1], sems.at[1]),
        pltpu.make_async_copy(latent, lat_buf, sems.at[2]),
    ]
    for copy in copies:
        copy.start()
    copies[2].wait()
    own = jnp.where(iota((16, 512), 1) // 64 == band, lat_buf[...].astype(f32), 0.0)
    pair = own[:, 0:128] + own[:, 128:256] + own[:, 256:384] + own[:, 384:512]
    left = (pair[:, 0:64] + pair[:, 64:128]).astype(bf16)
    for tap in range(2):
        copies[tap].wait()
        out[tap * 16 : tap * 16 + 16, :] = dot(left, tap_buf[tap]).astype(bf16)


def fold_taps(weight, latent_rows):
    taps, outs, ins = weight.shape
    lats = latent_rows.shape[0]
    whole = pl.BlockSpec(memory_space=pl.ANY)
    return pl.pallas_call(
        fold_kernel,
        in_specs=[whole, whole],
        out_specs=pl.BlockSpec(memory_space=pltpu.VMEM),
        out_shape=jax.ShapeDtypeStruct((2 * lats, ins), bf16),
        scratch_shapes=[
            pltpu.VMEM((2, outs, ins), bf16),
            pltpu.VMEM((lats, ins), bf16),
            pltpu.SemaphoreType.DMA((3,)),
        ],
        compiler_params=pltpu.CompilerParams(vmem_limit_bytes=56 * MIB),
        cost_estimate=pl.CostEstimate(flops=10**6, bytes_accessed=150000, transcendentals=0),
        name="fold_taps",
    )(weight, latent_rows)


def prep_kernel(main, prev, lat, cbias, lbias, act, base):
    def silu(value):
        value = value.astype(f32)
        half = 0.5 * value
        return (half * jnp.tanh(half) + half).astype(bf16)

    for frame in range(6):
        rows = prev[frame] if frame < 2 else main[frame - 2]
        act[frame * 128 : frame * 128 + 128, :] = silu(rows.reshape(128, 512))
    weight = lat[...]
    const = jnp.sum(weight.astype(f32) * cbias[...], axis=1, keepdims=True) + lbias[...]
    for frame in range(4):
        own = main[frame].reshape(128, 512)
        base[:, frame * 128 : frame * 128 + 128] = dot(weight, own, NT) + const


def prepare(video, prev, lat, conv_bias, latent_bias):
    return pl.pallas_call(
        prep_kernel,
        out_shape=(
            jax.ShapeDtypeStruct((768, 512), bf16),
            jax.ShapeDtypeStruct((16, 512), f32),
        ),
        compiler_params=pltpu.CompilerParams(vmem_limit_bytes=8 * MIB),
        cost_estimate=pl.CostEstimate(flops=2 * 10**7, bytes_accessed=3 * 10**6, transcendentals=800000),
        name="prepare",
    )(video, prev, lat, conv_bias.reshape(1, -1), latent_bias.reshape(-1, 1))


def conv_kernel(table, act, near, far1, far2, far3, base, own, first, second, weight, taps):
    even = lax.axis_index("head") % 2 == 0
    chip = lax.axis_index("seq") // 2
    for high, group in enumerate((near, far1, far2, far3)):
        for low in range(4):
            at = pl.multiple_of((chip ^ (high * 4 + low)) * 32, 32)
            weight[pl.ds(at, 32), :] = group[low]
    for frame in range(6):
        taps[frame] = dot(weight[0:432, :], act[frame * 128 : frame * 128 + 128, :], NT)
    column = iota((16, 128), 1) % 64

    def across(parts):
        left = jnp.where(column == 0, 0.0, pltpu.roll(parts[0], 1, 1))
        right = jnp.where(column == 63, 0.0, pltpu.roll(parts[2], 127, 1))
        return parts[1] + left + right

    upper = iota((16, 128), 1) < 64
    for frame in range(4):
        total = None
        for delay in range(3):
            part = taps[table[frame * 3 + delay], delay * 144 : delay * 144 + 144, :]
            total = part if total is None else total + part
        step = [
            across([total[(a * 3 + col) * 16 : (a * 3 + col) * 16 + 16] for col in range(3)])
            for a in range(3)
        ]
        from_above = jnp.where(upper, 0.0, pltpu.roll(step[0], 64, 1))
        from_below = jnp.where(upper, pltpu.roll(step[2], 64, 1), 0.0)
        here = slice(frame * 128, frame * 128 + 128)
        own[:, here] = base[:, here] + step[1] + from_above + from_below
        half = slice(frame * 64, frame * 64 + 64)
        above, below = step[2][:, 0:64], step[0][:, 64:128]
        first[:, half] = jnp.where(even, below, above)
        second[:, half] = jnp.where(even, above, below)


def convolve(table, act, folded, base):
    smem = pl.BlockSpec(memory_space=pltpu.SMEM)
    vmem = pl.BlockSpec(memory_space=pltpu.VMEM)
    return pl.pallas_call(
        conv_kernel,
        in_specs=[smem] + [vmem] * 6,
        out_specs=(vmem, vmem, vmem),
        out_shape=(
            jax.ShapeDtypeStruct((16, 512), f32),
            jax.ShapeDtypeStruct((16, 256), f32),
            jax.ShapeDtypeStruct((16, 256), f32),
        ),
        scratch_shapes=[pltpu.VMEM((512, 512), bf16), pltpu.VMEM((6, 432, 128), f32)],
        compiler_params=pltpu.CompilerParams(vmem_limit_bytes=10 * MIB),
        cost_estimate=pl.CostEstimate(flops=4 * 10**8, bytes_accessed=2 * 10**6, transcendentals=0),
        name="convolve",
    )(table, act, *folded, base)


def finish_kernel(own, first, second, out):
    even = lax.axis_index("head") % 2 == 0
    lane = iota((16, 128), 1)
    row = iota((128, 128), 0)
    pos = iota((128, 128), 1)
    own_half = (pos % 64) // 32 == row // 64
    own_cell = (pos // 64) * 2 + pos % 2 == row % 4
    keep = own_half & own_cell
    repeat = (iota((128, 16), 0) % 64 // 4 == iota((128, 16), 1)).astype(bf16)
    pick = ((lane % 32) // 2 == iota((16, 128), 0)).astype(bf16)
    for frame in range(4):
        half = slice(frame * 64, frame * 64 + 64)
        one, two = first[:, half], second[:, half]
        edge = jnp.concatenate([jnp.where(even, two, one), jnp.where(even, one, two)], axis=1)
        latent = ((own[:, frame * 128 : frame * 128 + 128] + edge) * latent_scale).astype(bf16)
        wide = jnp.where(keep, dot(repeat, latent), 0.0).astype(bf16)
        out[frame] = dot(pick, wide, NT).astype(bf16)


def finish(own, first, second):
    vmem = pl.BlockSpec(memory_space=pltpu.VMEM)
    return pl.pallas_call(
        finish_kernel,
        in_specs=[vmem, vmem, vmem],
        out_specs=vmem,
        out_shape=jax.ShapeDtypeStruct((4, 16, 128), bf16),
        compiler_params=pltpu.CompilerParams(vmem_limit_bytes=6 * MIB),
        cost_estimate=pl.CostEstimate(flops=10**7, bytes_accessed=10**6, transcendentals=0),
        name="finish",
    )(own, first, second)


def route_kernel(table, near, far1, far2, far3, mine, other, frames):
    seq = lax.axis_index("seq")
    chip, core = seq // 2, seq % 2
    for high, group in enumerate((near, far1, far2, far3)):
        for low in range(4):
            frames[high * 4 + low] = group[low]
    for out, owner in ((mine, core), (other, 1 - core)):
        for slot in range(4):
            frame = table[12 + owner * 4 + slot]
            here = (frame // 4) % 2 == core
            piece = frames[(frame // 8) ^ chip, frame % 4]
            out[slot] = jnp.where(here, piece, jnp.zeros_like(piece))


def route(table, groups):
    smem = pl.BlockSpec(memory_space=pltpu.SMEM)
    vmem = pl.BlockSpec(memory_space=pltpu.VMEM)
    shape = jax.ShapeDtypeStruct((4, 16, 128), bf16)
    return pl.pallas_call(
        route_kernel,
        in_specs=[smem] + [vmem] * 4,
        out_specs=(vmem, vmem),
        out_shape=(shape, shape),
        scratch_shapes=[pltpu.VMEM((16, 4, 16, 128), bf16)],
        compiler_params=pltpu.CompilerParams(vmem_limit_bytes=4 * MIB),
        cost_estimate=pl.CostEstimate(flops=1, bytes_accessed=10**6, transcendentals=0),
        name="route",
    )(table, *groups)


def scale_kernel(member, modulation, embed, bias, left, gram, gvec):
    width = embed.shape[1]
    chunk = 512
    mean = jnp.sum(embed[...].astype(f32), axis=1, keepdims=True) / width
    bias_mean = jnp.sum(bias[...], axis=1, keepdims=True) / width
    whole = jnp.zeros((80, 80), f32)
    for at in range(0, width, chunk):
        here = slice(at, at + chunk)
        centred = embed[:, here].astype(f32) - mean
        cbias = bias[:, here] - bias_mean
        scale = 1.0 + dot(member[...], modulation[:, width + at : width + at + chunk])
        shift = dot(member[...], modulation[:, here])
        first, second = scale[0:1], scale[1:2]
        high, low = split2(centred * first)
        left[0:64, here] = high
        left[64:128, here] = low
        high, low = split2(centred * second)
        left[128:192, here] = high
        left[192:256, here] = low
        high, low = split2(jnp.concatenate([cbias * first, cbias * second], axis=0))
        left[256:272, here] = jnp.concatenate(
            [high.astype(f32), low.astype(f32), shift[0:2], jnp.zeros((10, chunk), f32)], axis=0
        ).astype(bf16)
        full = jnp.concatenate([centred, cbias, jnp.zeros((15, chunk), f32)], axis=0)
        high, low = split2(full)
        whole = whole + (dot(high, high, NT) + dot(high, low, NT) + dot(low, high, NT))
    whole = whole * (1.0 / width)
    square = whole[0:64, 0:64]
    blank = jnp.zeros((64, 64), f32)
    block = jnp.concatenate(
        [jnp.concatenate([square, blank], axis=1), jnp.concatenate([blank, square], axis=1)], axis=0
    )
    top = block.astype(bf16)
    rest = block - top.astype(f32)
    mid = rest.astype(bf16)
    gram[0] = top
    gram[1] = mid
    gram[2] = (rest - mid.astype(f32)).astype(bf16)
    cross = 2.0 * whole[64:65, 0:64]
    const = jnp.broadcast_to(whole[64:65, 64:65], (1, 128))
    gvec[...] = jnp.concatenate(
        [jnp.concatenate([cross, cross], axis=1), const, jnp.zeros((6, 128), f32)], axis=0
    )


def scale_embedding(member, modulation, embed_weight, embed_bias):
    width = embed_weight.shape[1]
    vmem = pl.BlockSpec(memory_space=pltpu.VMEM)
    return pl.pallas_call(
        scale_kernel,
        in_specs=[vmem] * 4,
        out_specs=[vmem] * 3,
        out_shape=[
            jax.ShapeDtypeStruct((272, width), bf16),
            jax.ShapeDtypeStruct((3, 128, 128), bf16),
            jax.ShapeDtypeStruct((8, 128), f32),
        ],
        compiler_params=pltpu.CompilerParams(vmem_limit_bytes=8 * MIB),
        cost_estimate=pl.CostEstimate(flops=10**8, bytes_accessed=3 * 10**6, transcendentals=0),
        name="scale_embedding",
    )(member, modulation, embed_weight, embed_bias.reshape(1, -1))


def mix_kernel(left, qkv_w, qkv_b, mix, rows):
    product = dot(left[...], qkv_w[...])
    cols = product.shape[1]
    empty = jnp.zeros((64, cols), bf16)
    for clip in range(2):
        at = clip * 128
        high, low = split2(product[at : at + 64] + product[at + 64 : at + 128])
        mix[clip, 0] = jnp.concatenate([high, empty, low, empty], axis=0)
        mix[clip, 1] = jnp.concatenate([empty, high, empty, low], axis=0)
    tail = product[256:272]
    rows[...] = jnp.concatenate(
        [tail[0:2] + tail[2:4], tail[4:6] + qkv_b[...], jnp.zeros((4, cols), f32)], axis=0
    )


def mix_weights(left, qkv_weight, qkv_bias):
    width = left.shape[1]
    cols = 256
    return pl.pallas_call(
        mix_kernel,
        grid=(qkv_weight.shape[1] // cols,),
        in_specs=[
            pl.BlockSpec(left.shape, lambda n: (0, 0)),
            pl.BlockSpec((width, cols), lambda n: (0, n)),
            pl.BlockSpec((1, cols), lambda n: (0, n)),
        ],
        out_specs=[
            pl.BlockSpec((2, 2, 256, cols), lambda n: (0, 0, 0, n)),
            pl.BlockSpec((8, cols), lambda n: (0, n)),
        ],
        out_shape=[
            jax.ShapeDtypeStruct((2, 2, 256, 768), bf16),
            jax.ShapeDtypeStruct((8, 768), f32),
        ],
        compiler_params=pltpu.CompilerParams(vmem_limit_bytes=12 * MIB),
        cost_estimate=pl.CostEstimate(flops=13 * 10**8, bytes_accessed=6 * 10**6, transcendentals=0),
        name="mix_weights",
    )(left, qkv_weight, qkv_bias.reshape(1, -1))


def project(lead, own, mix, rows, gram, gvec, q_gain, k_gain, write):
    factor = math.log2(math.e) / math.sqrt(128)
    gains = q_gain[...] * factor, k_gain[...]
    count = own.shape[0]
    later = iota((count, 1), 0) // 16 % 4 >= lead
    twice = jnp.concatenate([own, own], axis=1)
    spread = dot(own, gram[0]) + dot(own, gram[1]) + dot(own, gram[2])
    terms = (spread + gvec[0:1, :]) * own.astype(f32)
    low_lane = iota((count, 128), 1) < 64
    slope = jnp.where(later, rows[1:2, :], rows[0:1, :])
    offset = jnp.where(later, rows[3:4, :], rows[2:3, :])
    for half in range(2):
        mine = jnp.where(low_lane == (half == 0), terms, 0.0)
        variance = jnp.sum(mine, axis=1, keepdims=True) + gvec[1:2, 0:1]
        scale = lax.rsqrt(jnp.maximum(variance, 0.0) + norm_eps)
        mixed = jnp.where(later, dot(twice, mix[1, half]), dot(twice, mix[0, half]))
        qkv = scale * (mixed + slope) + offset
        for head in range(2):
            at = head * 384
            for kind in range(2):
                part = qkv[:, at + kind * 128 : at + kind * 128 + 128]
                norm = lax.rsqrt(jnp.mean(part * part, axis=1, keepdims=True) + norm_eps)
                write(kind, head, half, (part * norm * gains[kind]).astype(bf16))
            write(2, head, half, qkv[:, at + 256 : at + 384].astype(bf16))


def project_kernel(table, tokens, mix, rows, gram, gvec, q_gain, k_gain, out):
    bands = tokens.shape[0]

    def write(kind, head, half, value):
        for band in range(bands):
            for frame in range(4):
                at = (half * bands + band) * 16
                out[kind, head, frame, at : at + 16, :] = value[
                    (band * 4 + frame) * 16 : (band * 4 + frame) * 16 + 16
                ]

    own = tokens[...].reshape(bands * 64, 128)
    project(table[20], own, mix, rows, gram, gvec, q_gain, k_gain, write)


def project_near(table, tokens, mix, rows, gram, gvec, q_gain, k_gain):
    smem = pl.BlockSpec(memory_space=pltpu.SMEM)
    vmem = pl.BlockSpec(memory_space=pltpu.VMEM)
    return pl.pallas_call(
        project_kernel,
        in_specs=[smem] + [vmem] * 7,
        out_specs=vmem,
        out_shape=jax.ShapeDtypeStruct((3, 2, 4, 128, 128), bf16),
        compiler_params=pltpu.CompilerParams(vmem_limit_bytes=10 * MIB),
        cost_estimate=pl.CostEstimate(flops=2 * 10**8, bytes_accessed=2 * 10**6, transcendentals=0),
        name="project_near",
    )(table, tokens, mix, rows, gram, gvec, q_gain, k_gain)


def attend_kernel(
    table, near, far, mix, rows, gram, gvec, q_gain, k_gain, out, parts
):
    lead = table[20]
    own_band = lax.axis_index("head")
    for kind in range(3):
        for head in range(2):
            for frame in range(4):
                parts[kind, head, frame * 256 : frame * 256 + 128, :] = near[kind, head, frame]

    def write(kind, head, half, value):
        for band in range(4):
            for frame in range(4):
                at = frame * 256 + 128 + (half * 4 + band) * 16
                parts[kind, head, at : at + 16, :] = value[
                    (band * 4 + frame) * 16 : (band * 4 + frame) * 16 + 16
                ]

    own = far[...].reshape(256, 128)
    project(lead, own, mix, rows, gram, gvec, q_gain, k_gain, write)

    def group(begin, end):
        for head in range(2):
            key = parts[1, head, begin * 256 : end * 256, :]
            value = parts[2, head, begin * 256 : end * 256, :]
            for frame in range(begin, end):
                score = dot(parts[0, head, frame * 256 : frame * 256 + 256, :], key, NT)
                top = jnp.max(score, axis=1, keepdims=True)
                expo = jnp.exp2(score - top)
                total = jnp.sum(expo, axis=1, keepdims=True)
                result = (dot(expo.astype(bf16), value) / total).astype(bf16)
                lanes = slice(head * 128, head * 128 + 128)
                for half in range(2):
                    for place in range(8):
                        at = place // 4 * 128 + (half * 4 + place % 4) * 16
                        out[own_band ^ place, frame, half, :, lanes] = result[at : at + 16]

    for first in (1, 2, 3):

        @pl.when(lead == first)
        def _(first=first):
            group(0, first)
            group(first, 4)


def attend(table, near, far, mix, rows, gram, gvec, q_gain, k_gain):
    smem = pl.BlockSpec(memory_space=pltpu.SMEM)
    vmem = pl.BlockSpec(memory_space=pltpu.VMEM)
    return pl.pallas_call(
        attend_kernel,
        in_specs=[smem] + [vmem] * 8,
        out_specs=vmem,
        out_shape=jax.ShapeDtypeStruct((8, 4, 2, 16, 256), bf16),
        scratch_shapes=[pltpu.VMEM((3, 2, 1024, 128), bf16)],
        compiler_params=pltpu.CompilerParams(vmem_limit_bytes=14 * MIB),
        cost_estimate=pl.CostEstimate(flops=10**9, bytes_accessed=3 * 10**6, transcendentals=1300000),
        name="attend",
    )(table, near, far, mix, rows, gram, gvec, q_gain, k_gain)


def neighbour(value, axis, step):
    count = lax.axis_size(axis)
    pairs = [(i, i + step) for i in range(count) if 0 <= i + step < count]
    return lax.ppermute(value, axis, pairs)


def swap(value, axis, mask):
    return lax.ppermute(value, axis, [(i, i ^ mask) for i in range(lax.axis_size(axis))])


def swap_pairs(value, axis, begin):
    pairs = [(i, i + 1) for i in range(begin, lax.axis_size(axis) - 1, 2)]
    return lax.ppermute(value, axis, pairs + [(b, a) for a, b in pairs])


def swap3(value, axis, unit):
    return [value] + [swap(value, axis, unit * step) for step in (3, 2, 1)][::-1]


def gather_chips(value):
    row = jnp.stack(swap3(value, "seq", 2))
    return swap3(row, "seq", 8)


def per_device(
    video_feat,
    clip_frames,
    clip_offset,
    conv_weight,
    conv_bias,
    latent_weight,
    latent_bias,
    embed_weight,
    embed_bias,
    modulation,
    qkv_weight,
    qkv_bias,
    q_gain,
    k_gain,
):
    seqs, heads = lax.axis_size("seq"), lax.axis_size("head")
    seq = lax.axis_index("seq")
    frames = video_feat.shape[0]
    latent_rows = latent_weight.T

    weight = conv_weight.transpose(0, 1, 2, 4, 3).reshape(27, conv_weight.shape[4], -1)
    part = fold_taps(weight, latent_rows)
    prev = neighbour(video_feat[2:], "seq", 1)
    add = lambda values: sum(value.astype(f32) for value in values).astype(bf16)
    four = add(swap3(part, "head", 1))
    taps = add([four, swap(four, "head", 4)])

    count = clip_frames.shape[0]
    numbers = jnp.arange(count, dtype=jnp.int32)
    starts = jnp.sum(jnp.where(numbers[None, :] < numbers[:, None], clip_frames[None, :], 0), axis=1)
    ids = seq * frames + jnp.arange(frames, dtype=jnp.int32)
    first = jnp.max(jnp.where(starts[None, :] <= ids[:, None], starts[None, :], 0), axis=1)
    slot = seq // 2 * 2 * frames + jnp.arange(2 * frames, dtype=jnp.int32)
    inside = (clip_offset[None, :] <= slot[:, None]) & (
        slot[:, None] < (clip_offset + clip_frames)[None, :]
    )
    origin = jnp.sum(jnp.where(inside, (starts - clip_offset)[None, :] + slot[:, None], 0), axis=1)
    origin = jnp.clip(origin, 0, seqs * frames - 1)
    delays = jnp.arange(3, dtype=jnp.int32)
    source = jnp.maximum(ids[:, None] - 2 + delays[None, :], first[:, None]) - seq * frames + 2
    source = jnp.clip(source, 0, frames + 1).reshape(-1)
    leading = clip_offset == seq * frames
    lead = jnp.sum(jnp.where(leading, clip_frames, 0)).reshape(1)
    table = jnp.concatenate([source, origin, lead])
    trailing = (clip_offset > seq * frames) & (clip_offset < (seq + 1) * frames)
    member = jnp.concatenate(
        [leading[None], trailing[None], jnp.zeros((6, count), jnp.bool_)], axis=0
    ).astype(bf16)

    left, gram, gvec = scale_embedding(member, modulation, embed_weight, embed_bias)

    taps, table, prev = lax.optimization_barrier((taps, table, prev))
    row = jnp.stack(swap3(taps, "seq", 2))
    folded = swap3(row, "seq", 8)
    mix, rows = mix_weights(left, qkv_weight, qkv_bias)
    mixed = mix, rows, gram, gvec
    act, base = prepare(video_feat, prev, latent_rows, conv_bias, latent_bias)

    own, first, second = convolve(table, act, folded, base)
    first = swap_pairs(first, "head", 0)
    second = swap_pairs(second, "head", 1)
    pieces = finish(own, first, second)

    mine, other = route(table, gather_chips(pieces))
    mine, other, mixed = lax.optimization_barrier((mine, other, mixed))
    slots = mine + swap(other, "seq", 1)
    near = jnp.stack(swap3(slots, "head", 1))
    far = swap(near, "head", 4)
    gains = q_gain.reshape(1, -1), k_gain.reshape(1, -1)
    ready = project_near(table, near, *mixed, *gains)
    out = attend(table, ready, far, *mixed, *gains)
    return out.reshape(heads * frames * 32, 256)


def solution(mesh):
    placed = (
        P("seq", "head", None, None),
        P(),
        P(),
        P(None, None, None, None, "head"),
        P(),
        P(),
        P(),
        P(),
        P(),
        P(),
        P(None, "head"),
        P("head"),
        P(),
        P(),
    )
    return jax.shard_map(
        per_device, mesh=mesh, in_specs=placed, out_specs=P("seq", "head"), check_vma=False
    )
```

```python
import functools
import math

import jax
import jax.numpy as jnp
from jax import lax
from jax.experimental import pallas as pl
from jax.experimental.pallas import tpu as pltpu
from jax.sharding import PartitionSpec as P

latent_scale = 0.476986
norm_eps = 1e-06
f32 = jnp.float32
bf16 = jnp.bfloat16
MIB = 1024 * 1024
NT = (((1,), (1,)), ((), ()))


def dot(a, b, dims=(((1,), (0,)), ((), ()))):
    return lax.dot_general(a, b, dims, preferred_element_type=f32)


def split2(value):
    high = value.astype(bf16)
    return high, (value - high.astype(f32)).astype(bf16)


def iota(shape, dim):
    return lax.broadcasted_iota(jnp.int32, shape, dim)


def fold_kernel(weight, latent, out, tap_buf, lat_buf, sems):
    band = lax.axis_index("head")
    tap = jnp.minimum(lax.axis_index("seq"), weight.shape[0] - 1)
    first = pltpu.make_async_copy(weight.at[tap], tap_buf, sems.at[0])
    second = pltpu.make_async_copy(latent, lat_buf, sems.at[1])
    first.start()
    second.start()
    second.wait()
    own = jnp.where(iota((16, 512), 1) // 64 == band, lat_buf[...].astype(f32), 0.0)
    pair = own[:, 0:128] + own[:, 128:256] + own[:, 256:384] + own[:, 384:512]
    left = (pair[:, 0:64] + pair[:, 64:128]).astype(bf16)
    first.wait()
    part = dot(left, tap_buf[...]).astype(bf16)
    for peer in range(out.shape[0]):
        out[peer] = part


def fold_tap(weight, latent_rows, copies):
    taps, outs, ins = weight.shape
    lats = latent_rows.shape[0]
    whole = pl.BlockSpec(memory_space=pl.ANY)
    return pl.pallas_call(
        fold_kernel,
        in_specs=[whole, whole],
        out_specs=pl.BlockSpec(memory_space=pltpu.VMEM),
        out_shape=jax.ShapeDtypeStruct((copies, lats, ins), bf16),
        scratch_shapes=[
            pltpu.VMEM((outs, ins), bf16),
            pltpu.VMEM((lats, ins), bf16),
            pltpu.SemaphoreType.DMA((2,)),
        ],
        compiler_params=pltpu.CompilerParams(vmem_limit_bytes=56 * MIB),
        cost_estimate=pl.CostEstimate(flops=10**6, bytes_accessed=150000, transcendentals=0),
        name="fold_tap",
    )(weight, latent_rows)


def prep_kernel(main, prev, lat, cbias, lbias, act, base):
    def silu(value):
        value = value.astype(f32)
        half = 0.5 * value
        return (half * jnp.tanh(half) + half).astype(bf16)

    for frame in range(6):
        rows = prev[frame] if frame < 2 else main[frame - 2]
        act[frame * 128 : frame * 128 + 128, :] = silu(rows.reshape(128, 512))
    weight = lat[...]
    const = jnp.sum(weight.astype(f32) * cbias[...], axis=1, keepdims=True) + lbias[...]
    for frame in range(4):
        own = main[frame].reshape(128, 512)
        base[:, frame * 128 : frame * 128 + 128] = dot(weight, own, NT) + const


def prepare(video, prev, lat, conv_bias, latent_bias):
    return pl.pallas_call(
        prep_kernel,
        out_shape=(
            jax.ShapeDtypeStruct((768, 512), bf16),
            jax.ShapeDtypeStruct((16, 512), f32),
        ),
        compiler_params=pltpu.CompilerParams(vmem_limit_bytes=8 * MIB),
        cost_estimate=pl.CostEstimate(flops=2 * 10**7, bytes_accessed=3 * 10**6, transcendentals=800000),
        name="prepare",
    )(video, prev, lat, conv_bias.reshape(1, -1), latent_bias.reshape(-1, 1))


def conv_kernel(table, act, same, other, base, own, first, second, weight, taps):
    even = lax.axis_index("head") % 2 == 0
    core = lax.axis_index("seq") % 2
    for chip in range(16):
        own_at = pl.multiple_of(chip * 32 + core * 16, 16)
        pair_at = pl.multiple_of(chip * 32 + 16 - core * 16, 16)
        weight[pl.ds(own_at, 16), :] = same[chip]
        weight[pl.ds(pair_at, 16), :] = other[chip]
    for frame in range(6):
        taps[frame] = dot(weight[0:432, :], act[frame * 128 : frame * 128 + 128, :], NT)
    column = iota((16, 128), 1) % 64

    def across(parts):
        left = jnp.where(column == 0, 0.0, pltpu.roll(parts[0], 1, 1))
        right = jnp.where(column == 63, 0.0, pltpu.roll(parts[2], 127, 1))
        return parts[1] + left + right

    upper = iota((16, 128), 1) < 64
    for frame in range(4):
        total = None
        for delay in range(3):
            part = taps[table[frame * 3 + delay], delay * 144 : delay * 144 + 144, :]
            total = part if total is None else total + part
        step = [
            across([total[(a * 3 + col) * 16 : (a * 3 + col) * 16 + 16] for col in range(3)])
            for a in range(3)
        ]
        from_above = jnp.where(upper, 0.0, pltpu.roll(step[0], 64, 1))
        from_below = jnp.where(upper, pltpu.roll(step[2], 64, 1), 0.0)
        here = slice(frame * 128, frame * 128 + 128)
        own[:, here] = base[:, here] + step[1] + from_above + from_below
        half = slice(frame * 64, frame * 64 + 64)
        above, below = step[2][:, 0:64], step[0][:, 64:128]
        first[:, half] = jnp.where(even, below, above)
        second[:, half] = jnp.where(even, above, below)


def convolve(table, act, folded, base):
    smem = pl.BlockSpec(memory_space=pltpu.SMEM)
    vmem = pl.BlockSpec(memory_space=pltpu.VMEM)
    return pl.pallas_call(
        conv_kernel,
        in_specs=[smem] + [vmem] * 4,
        out_specs=(vmem, vmem, vmem),
        out_shape=(
            jax.ShapeDtypeStruct((16, 512), f32),
            jax.ShapeDtypeStruct((16, 256), f32),
            jax.ShapeDtypeStruct((16, 256), f32),
        ),
        scratch_shapes=[pltpu.VMEM((512, 512), bf16), pltpu.VMEM((6, 432, 128), f32)],
        compiler_params=pltpu.CompilerParams(vmem_limit_bytes=10 * MIB),
        cost_estimate=pl.CostEstimate(flops=4 * 10**8, bytes_accessed=2 * 10**6, transcendentals=0),
        name="convolve",
    )(table, act, *folded, base)


def finish_kernel(own, first, second, out):
    even = lax.axis_index("head") % 2 == 0
    lane = iota((16, 128), 1)
    row = iota((128, 128), 0)
    pos = iota((128, 128), 1)
    own_half = (pos % 64) // 32 == row // 64
    own_cell = (pos // 64) * 2 + pos % 2 == row % 4
    keep = own_half & own_cell
    repeat = (iota((128, 16), 0) % 64 // 4 == iota((128, 16), 1)).astype(bf16)
    pick = ((lane % 32) // 2 == iota((16, 128), 0)).astype(bf16)
    for frame in range(4):
        half = slice(frame * 64, frame * 64 + 64)
        one, two = first[:, half], second[:, half]
        edge = jnp.concatenate([jnp.where(even, two, one), jnp.where(even, one, two)], axis=1)
        latent = ((own[:, frame * 128 : frame * 128 + 128] + edge) * latent_scale).astype(bf16)
        wide = jnp.where(keep, dot(repeat, latent), 0.0).astype(bf16)
        piece = dot(pick, wide, NT).astype(bf16)
        for peer in range(out.shape[0]):
            out[peer, frame] = piece


def finish(own, first, second, copies):
    vmem = pl.BlockSpec(memory_space=pltpu.VMEM)
    return pl.pallas_call(
        finish_kernel,
        in_specs=[vmem, vmem, vmem],
        out_specs=vmem,
        out_shape=jax.ShapeDtypeStruct((copies, 4, 16, 128), bf16),
        compiler_params=pltpu.CompilerParams(vmem_limit_bytes=6 * MIB),
        cost_estimate=pl.CostEstimate(flops=10**7, bytes_accessed=10**6, transcendentals=0),
        name="finish",
    )(own, first, second)


def route_kernel(table, frames, mine, other):
    core = lax.axis_index("seq") % 2
    for out, owner in ((mine, core), (other, 1 - core)):
        for slot in range(4):
            frame = table[12 + owner * 4 + slot]
            here = (frame // 4) % 2 == core
            piece = frames[frame // 8, frame % 4]
            out[slot] = jnp.where(here, piece, jnp.zeros_like(piece))


def route(table, frames):
    smem = pl.BlockSpec(memory_space=pltpu.SMEM)
    vmem = pl.BlockSpec(memory_space=pltpu.VMEM)
    shape = jax.ShapeDtypeStruct((4, 16, 128), bf16)
    return pl.pallas_call(
        route_kernel,
        in_specs=[smem, vmem],
        out_specs=(vmem, vmem),
        out_shape=(shape, shape),
        compiler_params=pltpu.CompilerParams(vmem_limit_bytes=4 * MIB),
        cost_estimate=pl.CostEstimate(flops=1, bytes_accessed=10**6, transcendentals=0),
        name="route",
    )(table, frames)


def scale_kernel(member, modulation, embed, bias, left, gram, gvec):
    width = embed.shape[1]
    chunk = 512
    mean = jnp.sum(embed[...].astype(f32), axis=1, keepdims=True) / width
    bias_mean = jnp.sum(bias[...], axis=1, keepdims=True) / width
    whole = jnp.zeros((80, 80), f32)
    for at in range(0, width, chunk):
        here = slice(at, at + chunk)
        centred = embed[:, here].astype(f32) - mean
        cbias = bias[:, here] - bias_mean
        scale = 1.0 + dot(member[...], modulation[:, width + at : width + at + chunk])
        shift = dot(member[...], modulation[:, here])
        first, second = scale[0:1], scale[1:2]
        high, low = split2(centred * first)
        left[0:64, here] = high
        left[64:128, here] = low
        high, low = split2(centred * second)
        left[128:192, here] = high
        left[192:256, here] = low
        high, low = split2(jnp.concatenate([cbias * first, cbias * second], axis=0))
        left[256:272, here] = jnp.concatenate(
            [high.astype(f32), low.astype(f32), shift[0:2], jnp.zeros((10, chunk), f32)], axis=0
        ).astype(bf16)
        full = jnp.concatenate([centred, cbias, jnp.zeros((15, chunk), f32)], axis=0)
        high, low = split2(full)
        whole = whole + (dot(high, high, NT) + dot(high, low, NT) + dot(low, high, NT))
    whole = whole * (1.0 / width)
    square = whole[0:64, 0:64]
    blank = jnp.zeros((64, 64), f32)
    block = jnp.concatenate(
        [jnp.concatenate([square, blank], axis=1), jnp.concatenate([blank, square], axis=1)], axis=0
    )
    top = block.astype(bf16)
    rest = block - top.astype(f32)
    mid = rest.astype(bf16)
    gram[0] = top
    gram[1] = mid
    gram[2] = (rest - mid.astype(f32)).astype(bf16)
    cross = 2.0 * whole[64:65, 0:64]
    const = jnp.broadcast_to(whole[64:65, 64:65], (1, 128))
    gvec[...] = jnp.concatenate(
        [jnp.concatenate([cross, cross], axis=1), const, jnp.zeros((6, 128), f32)], axis=0
    )


def scale_embedding(member, modulation, embed_weight, embed_bias):
    width = embed_weight.shape[1]
    vmem = pl.BlockSpec(memory_space=pltpu.VMEM)
    return pl.pallas_call(
        scale_kernel,
        in_specs=[vmem] * 4,
        out_specs=[vmem] * 3,
        out_shape=[
            jax.ShapeDtypeStruct((272, width), bf16),
            jax.ShapeDtypeStruct((3, 128, 128), bf16),
            jax.ShapeDtypeStruct((8, 128), f32),
        ],
        compiler_params=pltpu.CompilerParams(vmem_limit_bytes=8 * MIB),
        cost_estimate=pl.CostEstimate(flops=10**8, bytes_accessed=3 * 10**6, transcendentals=0),
        name="scale_embedding",
    )(member, modulation, embed_weight, embed_bias.reshape(1, -1))


def mix_kernel(left, qkv_w, qkv_b, mix, rows):
    product = dot(left[...], qkv_w[...])
    cols = product.shape[1]
    empty = jnp.zeros((64, cols), bf16)
    for clip in range(2):
        at = clip * 128
        high, low = split2(product[at : at + 64] + product[at + 64 : at + 128])
        mix[clip, 0] = jnp.concatenate([high, empty, low, empty], axis=0)
        mix[clip, 1] = jnp.concatenate([empty, high, empty, low], axis=0)
    tail = product[256:272]
    rows[...] = jnp.concatenate(
        [tail[0:2] + tail[2:4], tail[4:6] + qkv_b[...], jnp.zeros((4, cols), f32)], axis=0
    )


def mix_weights(left, qkv_weight, qkv_bias):
    width = left.shape[1]
    cols = 256
    return pl.pallas_call(
        mix_kernel,
        grid=(qkv_weight.shape[1] // cols,),
        in_specs=[
            pl.BlockSpec(left.shape, lambda n: (0, 0)),
            pl.BlockSpec((width, cols), lambda n: (0, n)),
            pl.BlockSpec((1, cols), lambda n: (0, n)),
        ],
        out_specs=[
            pl.BlockSpec((2, 2, 256, cols), lambda n: (0, 0, 0, n)),
            pl.BlockSpec((8, cols), lambda n: (0, n)),
        ],
        out_shape=[
            jax.ShapeDtypeStruct((2, 2, 256, 768), bf16),
            jax.ShapeDtypeStruct((8, 768), f32),
        ],
        compiler_params=pltpu.CompilerParams(vmem_limit_bytes=12 * MIB),
        cost_estimate=pl.CostEstimate(flops=13 * 10**8, bytes_accessed=6 * 10**6, transcendentals=0),
        name="mix_weights",
    )(left, qkv_weight, qkv_bias.reshape(1, -1))


def project(lead, own, mix, rows, gram, gvec, q_gain, k_gain, write):
    factor = math.log2(math.e) / math.sqrt(128)
    gains = q_gain[...] * factor, k_gain[...]
    count = own.shape[0]
    later = iota((count, 1), 0) // 16 % 4 >= lead
    twice = jnp.concatenate([own, own], axis=1)
    spread = dot(own, gram[0]) + dot(own, gram[1]) + dot(own, gram[2])
    terms = (spread + gvec[0:1, :]) * own.astype(f32)
    low_lane = iota((count, 128), 1) < 64
    slope = jnp.where(later, rows[1:2, :], rows[0:1, :])
    offset = jnp.where(later, rows[3:4, :], rows[2:3, :])
    for half in range(2):
        mine = jnp.where(low_lane == (half == 0), terms, 0.0)
        variance = jnp.sum(mine, axis=1, keepdims=True) + gvec[1:2, 0:1]
        scale = lax.rsqrt(jnp.maximum(variance, 0.0) + norm_eps)
        mixed = jnp.where(later, dot(twice, mix[1, half]), dot(twice, mix[0, half]))
        qkv = scale * (mixed + slope) + offset
        for head in range(2):
            at = head * 384
            for kind in range(2):
                part = qkv[:, at + kind * 128 : at + kind * 128 + 128]
                norm = lax.rsqrt(jnp.mean(part * part, axis=1, keepdims=True) + norm_eps)
                write(kind, head, half, (part * norm * gains[kind]).astype(bf16))
            write(2, head, half, qkv[:, at + 256 : at + 384].astype(bf16))


def project_kernel(table, tokens, mix, rows, gram, gvec, q_gain, k_gain, out):
    bands = tokens.shape[0]

    def write(kind, head, half, value):
        for band in range(bands):
            for frame in range(4):
                at = (half * bands + band) * 16
                out[kind, head, frame, at : at + 16, :] = value[
                    (band * 4 + frame) * 16 : (band * 4 + frame) * 16 + 16
                ]

    own = tokens[...].reshape(bands * 64, 128)
    project(table[20], own, mix, rows, gram, gvec, q_gain, k_gain, write)


def project_near(table, tokens, mix, rows, gram, gvec, q_gain, k_gain):
    smem = pl.BlockSpec(memory_space=pltpu.SMEM)
    vmem = pl.BlockSpec(memory_space=pltpu.VMEM)
    return pl.pallas_call(
        project_kernel,
        in_specs=[smem] + [vmem] * 7,
        out_specs=vmem,
        out_shape=jax.ShapeDtypeStruct((3, 2, 4, 128, 128), bf16),
        compiler_params=pltpu.CompilerParams(vmem_limit_bytes=10 * MIB),
        cost_estimate=pl.CostEstimate(flops=2 * 10**8, bytes_accessed=2 * 10**6, transcendentals=0),
        name="project_near",
    )(table, tokens, mix, rows, gram, gvec, q_gain, k_gain)


def attend_kernel(
    table, near, far, mix, rows, gram, gvec, q_gain, k_gain, out, parts
):
    lead = table[20]
    own_band = lax.axis_index("head")
    for kind in range(3):
        for head in range(2):
            for frame in range(4):
                parts[kind, head, frame * 256 : frame * 256 + 128, :] = near[kind, head, frame]

    def write(kind, head, half, value):
        for band in range(4):
            for frame in range(4):
                at = frame * 256 + 128 + (half * 4 + band) * 16
                parts[kind, head, at : at + 16, :] = value[
                    (band * 4 + frame) * 16 : (band * 4 + frame) * 16 + 16
                ]

    own = far[...].reshape(256, 128)
    project(lead, own, mix, rows, gram, gvec, q_gain, k_gain, write)

    def group(begin, end):
        for head in range(2):
            key = parts[1, head, begin * 256 : end * 256, :]
            value = parts[2, head, begin * 256 : end * 256, :]
            for frame in range(begin, end):
                score = dot(parts[0, head, frame * 256 : frame * 256 + 256, :], key, NT)
                top = jnp.max(score, axis=1, keepdims=True)
                expo = jnp.exp2(score - top)
                total = jnp.sum(expo, axis=1, keepdims=True)
                result = (dot(expo.astype(bf16), value) / total).astype(bf16)
                lanes = slice(head * 128, head * 128 + 128)
                for half in range(2):
                    for place in range(8):
                        at = place // 4 * 128 + (half * 4 + place % 4) * 16
                        out[own_band ^ place, frame, half, :, lanes] = result[at : at + 16]

    for first in (1, 2, 3):

        @pl.when(lead == first)
        def _(first=first):
            group(0, first)
            group(first, 4)


def attend(table, near, far, mix, rows, gram, gvec, q_gain, k_gain):
    smem = pl.BlockSpec(memory_space=pltpu.SMEM)
    vmem = pl.BlockSpec(memory_space=pltpu.VMEM)
    return pl.pallas_call(
        attend_kernel,
        in_specs=[smem] + [vmem] * 8,
        out_specs=vmem,
        out_shape=jax.ShapeDtypeStruct((8, 4, 2, 16, 256), bf16),
        scratch_shapes=[pltpu.VMEM((3, 2, 1024, 128), bf16)],
        compiler_params=pltpu.CompilerParams(vmem_limit_bytes=14 * MIB),
        cost_estimate=pl.CostEstimate(flops=10**9, bytes_accessed=3 * 10**6, transcendentals=1300000),
        name="attend",
    )(table, near, far, mix, rows, gram, gvec, q_gain, k_gain)


def neighbour(value, axis, step):
    count = lax.axis_size(axis)
    pairs = [(i, i + step) for i in range(count) if 0 <= i + step < count]
    return lax.ppermute(value, axis, pairs)


def swap(value, axis, mask):
    return lax.ppermute(value, axis, [(i, i ^ mask) for i in range(lax.axis_size(axis))])


def swap_pairs(value, axis, begin):
    pairs = [(i, i + 1) for i in range(begin, lax.axis_size(axis) - 1, 2)]
    return lax.ppermute(value, axis, pairs + [(b, a) for a, b in pairs])


def swap3(value, axis, unit):
    return [value] + [swap(value, axis, unit * step) for step in (3, 2, 1)][::-1]


def per_device(
    video_feat,
    clip_frames,
    clip_offset,
    conv_weight,
    conv_bias,
    latent_weight,
    latent_bias,
    embed_weight,
    embed_bias,
    modulation,
    qkv_weight,
    qkv_bias,
    q_gain,
    k_gain,
):
    seqs, heads = lax.axis_size("seq"), lax.axis_size("head")
    seq = lax.axis_index("seq")
    frames = video_feat.shape[0]
    latent_rows = latent_weight.T

    weight = conv_weight.transpose(0, 1, 2, 4, 3).reshape(27, conv_weight.shape[4], -1)
    parts = lax.all_to_all(fold_tap(weight, latent_rows, heads), "head", 0, 0)
    prev = neighbour(video_feat[2:], "seq", 1)
    tap = jnp.sum(parts.astype(f32), axis=0).astype(bf16)

    count = clip_frames.shape[0]
    numbers = jnp.arange(count, dtype=jnp.int32)
    starts = jnp.sum(jnp.where(numbers[None, :] < numbers[:, None], clip_frames[None, :], 0), axis=1)
    ids = seq * frames + jnp.arange(frames, dtype=jnp.int32)
    first = jnp.max(jnp.where(starts[None, :] <= ids[:, None], starts[None, :], 0), axis=1)
    slot = seq // 2 * 2 * frames + jnp.arange(2 * frames, dtype=jnp.int32)
    inside = (clip_offset[None, :] <= slot[:, None]) & (
        slot[:, None] < (clip_offset + clip_frames)[None, :]
    )
    origin = jnp.sum(jnp.where(inside, (starts - clip_offset)[None, :] + slot[:, None], 0), axis=1)
    origin = jnp.clip(origin, 0, seqs * frames - 1)
    delays = jnp.arange(3, dtype=jnp.int32)
    source = jnp.maximum(ids[:, None] - 2 + delays[None, :], first[:, None]) - seq * frames + 2
    source = jnp.clip(source, 0, frames + 1).reshape(-1)
    leading = clip_offset == seq * frames
    lead = jnp.sum(jnp.where(leading, clip_frames, 0)).reshape(1)
    table = jnp.concatenate([source, origin, lead])
    trailing = (clip_offset > seq * frames) & (clip_offset < (seq + 1) * frames)
    member = jnp.concatenate(
        [leading[None], trailing[None], jnp.zeros((6, count), jnp.bool_)], axis=0
    ).astype(bf16)

    left, gram, gvec = scale_embedding(member, modulation, embed_weight, embed_bias)

    tap, table, prev = lax.optimization_barrier((tap, table, prev))
    chips = seqs // 2
    cores = [[2 * chip + core for chip in range(chips)] for core in range(2)]
    over_chips = lambda value: lax.all_to_all(value, "seq", 0, 0, axis_index_groups=cores)
    same = over_chips(jnp.broadcast_to(tap[None], (chips,) + tap.shape))
    folded = same, swap(same, "seq", 1)
    mix, rows = mix_weights(left, qkv_weight, qkv_bias)
    mixed = mix, rows, gram, gvec
    act, base = prepare(video_feat, prev, latent_rows, conv_bias, latent_bias)

    own, first, second = convolve(table, act, folded, base)
    first = swap_pairs(first, "head", 0)
    second = swap_pairs(second, "head", 1)
    pieces = finish(own, first, second, chips)
    frames_all = over_chips(pieces)
    mine, other = route(table, frames_all)
    mine, other, mixed = lax.optimization_barrier((mine, other, mixed))
    slots = mine + swap(other, "seq", 1)
    near = jnp.stack(swap3(slots, "head", 1))
    far = swap(near, "head", 4)
    gains = q_gain.reshape(1, -1), k_gain.reshape(1, -1)
    ready = project_near(table, near, *mixed, *gains)
    out = attend(table, ready, far, *mixed, *gains)
    return out.reshape(heads * frames * 32, 256)


def solution(mesh):
    placed = (
        P("seq", "head", None, None),
        P(),
        P(),
        P(None, None, None, None, "head"),
        P(),
        P(),
        P(),
        P(),
        P(),
        P(),
        P(None, "head"),
        P("head"),
        P(),
        P(),
    )
    return jax.shard_map(
        per_device, mesh=mesh, in_specs=placed, out_specs=P("seq", "head"), check_vma=False
    )
```

```python
import functools
import math

import jax
import jax.numpy as jnp
from jax import lax
from jax.experimental import pallas as pl
from jax.experimental.pallas import tpu as pltpu
from jax.sharding import PartitionSpec as P

latent_scale = 0.476986
norm_eps = 1e-06
f32 = jnp.float32
bf16 = jnp.bfloat16
MIB = 1024 * 1024
NT = (((1,), (1,)), ((), ()))


def dot(a, b, dims=(((1,), (0,)), ((), ()))):
    return lax.dot_general(a, b, dims, preferred_element_type=f32)


def split2(value):
    high = value.astype(bf16)
    return high, (value - high.astype(f32)).astype(bf16)


def iota(shape, dim):
    return lax.broadcasted_iota(jnp.int32, shape, dim)


def fold_kernel(weight, latent, out, tap_buf, lat_buf, sems):
    band = lax.axis_index("head")
    tap = jnp.minimum(lax.axis_index("seq"), weight.shape[0] - 1)
    first = pltpu.make_async_copy(weight.at[tap], tap_buf, sems.at[0])
    second = pltpu.make_async_copy(latent, lat_buf, sems.at[1])
    first.start()
    second.start()
    second.wait()
    own = jnp.where(iota((16, 512), 1) // 64 == band, lat_buf[...].astype(f32), 0.0)
    pair = own[:, 0:128] + own[:, 128:256] + own[:, 256:384] + own[:, 384:512]
    left = (pair[:, 0:64] + pair[:, 64:128]).astype(bf16)
    first.wait()
    part = dot(left, tap_buf[...]).astype(bf16)
    for peer in range(out.shape[0]):
        out[peer] = part


def fold_tap(weight, latent_rows, copies):
    taps, outs, ins = weight.shape
    lats = latent_rows.shape[0]
    whole = pl.BlockSpec(memory_space=pl.ANY)
    return pl.pallas_call(
        fold_kernel,
        in_specs=[whole, whole],
        out_specs=pl.BlockSpec(memory_space=pltpu.VMEM),
        out_shape=jax.ShapeDtypeStruct((copies, lats, ins), bf16),
        scratch_shapes=[
            pltpu.VMEM((outs, ins), bf16),
            pltpu.VMEM((lats, ins), bf16),
            pltpu.SemaphoreType.DMA((2,)),
        ],
        compiler_params=pltpu.CompilerParams(vmem_limit_bytes=56 * MIB),
        cost_estimate=pl.CostEstimate(flops=10**6, bytes_accessed=150000, transcendentals=0),
        name="fold_tap",
    )(weight, latent_rows)


def prep_kernel(main, prev, lat, cbias, lbias, act, base):
    def silu(value):
        value = value.astype(f32)
        half = 0.5 * value
        return (half * jnp.tanh(half) + half).astype(bf16)

    for frame in range(6):
        rows = prev[frame] if frame < 2 else main[frame - 2]
        act[frame * 128 : frame * 128 + 128, :] = silu(rows.reshape(128, 512))
    weight = lat[...]
    const = jnp.sum(weight.astype(f32) * cbias[...], axis=1, keepdims=True) + lbias[...]
    for frame in range(4):
        own = main[frame].reshape(128, 512)
        base[:, frame * 128 : frame * 128 + 128] = dot(weight, own, NT) + const


def prepare(video, prev, lat, conv_bias, latent_bias):
    return pl.pallas_call(
        prep_kernel,
        out_shape=(
            jax.ShapeDtypeStruct((768, 512), bf16),
            jax.ShapeDtypeStruct((16, 512), f32),
        ),
        compiler_params=pltpu.CompilerParams(vmem_limit_bytes=8 * MIB),
        cost_estimate=pl.CostEstimate(flops=2 * 10**7, bytes_accessed=3 * 10**6, transcendentals=800000),
        name="prepare",
    )(video, prev, lat, conv_bias.reshape(1, -1), latent_bias.reshape(-1, 1))


def conv_kernel(table, act, same, other, base, own, first, second, weight, taps):
    even = lax.axis_index("head") % 2 == 0
    core = lax.axis_index("seq") % 2
    for chip in range(16):
        own_at = pl.multiple_of(chip * 32 + core * 16, 16)
        pair_at = pl.multiple_of(chip * 32 + 16 - core * 16, 16)
        weight[pl.ds(own_at, 16), :] = same[chip]
        weight[pl.ds(pair_at, 16), :] = other[chip]
    for frame in range(6):
        taps[frame] = dot(weight[0:432, :], act[frame * 128 : frame * 128 + 128, :], NT)
    column = iota((16, 128), 1) % 64

    def across(parts):
        left = jnp.where(column == 0, 0.0, pltpu.roll(parts[0], 1, 1))
        right = jnp.where(column == 63, 0.0, pltpu.roll(parts[2], 127, 1))
        return parts[1] + left + right

    upper = iota((16, 128), 1) < 64
    for frame in range(4):
        total = None
        for delay in range(3):
            part = taps[table[frame * 3 + delay], delay * 144 : delay * 144 + 144, :]
            total = part if total is None else total + part
        step = [
            across([total[(a * 3 + col) * 16 : (a * 3 + col) * 16 + 16] for col in range(3)])
            for a in range(3)
        ]
        from_above = jnp.where(upper, 0.0, pltpu.roll(step[0], 64, 1))
        from_below = jnp.where(upper, pltpu.roll(step[2], 64, 1), 0.0)
        here = slice(frame * 128, frame * 128 + 128)
        own[:, here] = base[:, here] + step[1] + from_above + from_below
        half = slice(frame * 64, frame * 64 + 64)
        above, below = step[2][:, 0:64], step[0][:, 64:128]
        first[:, half] = jnp.where(even, below, above)
        second[:, half] = jnp.where(even, above, below)


def convolve(table, act, folded, base):
    smem = pl.BlockSpec(memory_space=pltpu.SMEM)
    vmem = pl.BlockSpec(memory_space=pltpu.VMEM)
    return pl.pallas_call(
        conv_kernel,
        in_specs=[smem] + [vmem] * 4,
        out_specs=(vmem, vmem, vmem),
        out_shape=(
            jax.ShapeDtypeStruct((16, 512), f32),
            jax.ShapeDtypeStruct((16, 256), f32),
            jax.ShapeDtypeStruct((16, 256), f32),
        ),
        scratch_shapes=[pltpu.VMEM((512, 512), bf16), pltpu.VMEM((6, 432, 128), f32)],
        compiler_params=pltpu.CompilerParams(vmem_limit_bytes=10 * MIB),
        cost_estimate=pl.CostEstimate(flops=4 * 10**8, bytes_accessed=2 * 10**6, transcendentals=0),
        name="convolve",
    )(table, act, *folded, base)


def finish_kernel(own, first, second, out):
    even = lax.axis_index("head") % 2 == 0
    lane = iota((16, 128), 1)
    row = iota((128, 128), 0)
    pos = iota((128, 128), 1)
    own_half = (pos % 64) // 32 == row // 64
    own_cell = (pos // 64) * 2 + pos % 2 == row % 4
    keep = own_half & own_cell
    repeat = (iota((128, 16), 0) % 64 // 4 == iota((128, 16), 1)).astype(bf16)
    pick = ((lane % 32) // 2 == iota((16, 128), 0)).astype(bf16)
    for frame in range(4):
        half = slice(frame * 64, frame * 64 + 64)
        one, two = first[:, half], second[:, half]
        edge = jnp.concatenate([jnp.where(even, two, one), jnp.where(even, one, two)], axis=1)
        latent = ((own[:, frame * 128 : frame * 128 + 128] + edge) * latent_scale).astype(bf16)
        wide = jnp.where(keep, dot(repeat, latent), 0.0).astype(bf16)
        piece = dot(pick, wide, NT).astype(bf16)
        for peer in range(out.shape[0]):
            out[peer, frame] = piece


def finish(own, first, second, copies):
    vmem = pl.BlockSpec(memory_space=pltpu.VMEM)
    return pl.pallas_call(
        finish_kernel,
        in_specs=[vmem, vmem, vmem],
        out_specs=vmem,
        out_shape=jax.ShapeDtypeStruct((copies, 4, 16, 128), bf16),
        compiler_params=pltpu.CompilerParams(vmem_limit_bytes=6 * MIB),
        cost_estimate=pl.CostEstimate(flops=10**7, bytes_accessed=10**6, transcendentals=0),
        name="finish",
    )(own, first, second)


def route_kernel(table, frames, mine, other):
    core = lax.axis_index("seq") % 2
    for out, owner in ((mine, core), (other, 1 - core)):
        for slot in range(4):
            frame = table[12 + owner * 4 + slot]
            here = (frame // 4) % 2 == core
            piece = frames[frame // 8, frame % 4]
            out[slot] = jnp.where(here, piece, jnp.zeros_like(piece))


def route(table, frames):
    smem = pl.BlockSpec(memory_space=pltpu.SMEM)
    vmem = pl.BlockSpec(memory_space=pltpu.VMEM)
    shape = jax.ShapeDtypeStruct((4, 16, 128), bf16)
    return pl.pallas_call(
        route_kernel,
        in_specs=[smem, vmem],
        out_specs=(vmem, vmem),
        out_shape=(shape, shape),
        compiler_params=pltpu.CompilerParams(vmem_limit_bytes=4 * MIB),
        cost_estimate=pl.CostEstimate(flops=1, bytes_accessed=10**6, transcendentals=0),
        name="route",
    )(table, frames)


def scale_kernel(member, modulation, embed, bias, left, gram, gvec):
    width = embed.shape[1]
    chunk = 512
    mean = jnp.sum(embed[...].astype(f32), axis=1, keepdims=True) / width
    bias_mean = jnp.sum(bias[...], axis=1, keepdims=True) / width
    whole = jnp.zeros((80, 80), f32)
    for at in range(0, width, chunk):
        here = slice(at, at + chunk)
        centred = embed[:, here].astype(f32) - mean
        cbias = bias[:, here] - bias_mean
        scale = 1.0 + dot(member[...], modulation[:, width + at : width + at + chunk])
        shift = dot(member[...], modulation[:, here])
        first, second = scale[0:1], scale[1:2]
        high, low = split2(centred * first)
        left[0:64, here] = high
        left[64:128, here] = low
        high, low = split2(centred * second)
        left[128:192, here] = high
        left[192:256, here] = low
        high, low = split2(jnp.concatenate([cbias * first, cbias * second], axis=0))
        left[256:272, here] = jnp.concatenate(
            [high.astype(f32), low.astype(f32), shift[0:2], jnp.zeros((10, chunk), f32)], axis=0
        ).astype(bf16)
        full = jnp.concatenate([centred, cbias, jnp.zeros((15, chunk), f32)], axis=0)
        high, low = split2(full)
        whole = whole + (dot(high, high, NT) + dot(high, low, NT) + dot(low, high, NT))
    whole = whole * (1.0 / width)
    square = whole[0:64, 0:64]
    blank = jnp.zeros((64, 64), f32)
    block = jnp.concatenate(
        [jnp.concatenate([square, blank], axis=1), jnp.concatenate([blank, square], axis=1)], axis=0
    )
    top = block.astype(bf16)
    rest = block - top.astype(f32)
    mid = rest.astype(bf16)
    gram[0] = top
    gram[1] = mid
    gram[2] = (rest - mid.astype(f32)).astype(bf16)
    cross = 2.0 * whole[64:65, 0:64]
    const = jnp.broadcast_to(whole[64:65, 64:65], (1, 128))
    gvec[...] = jnp.concatenate(
        [jnp.concatenate([cross, cross], axis=1), const, jnp.zeros((6, 128), f32)], axis=0
    )


def scale_embedding(member, modulation, embed_weight, embed_bias):
    width = embed_weight.shape[1]
    vmem = pl.BlockSpec(memory_space=pltpu.VMEM)
    return pl.pallas_call(
        scale_kernel,
        in_specs=[vmem] * 4,
        out_specs=[vmem] * 3,
        out_shape=[
            jax.ShapeDtypeStruct((272, width), bf16),
            jax.ShapeDtypeStruct((3, 128, 128), bf16),
            jax.ShapeDtypeStruct((8, 128), f32),
        ],
        compiler_params=pltpu.CompilerParams(vmem_limit_bytes=8 * MIB),
        cost_estimate=pl.CostEstimate(flops=10**8, bytes_accessed=3 * 10**6, transcendentals=0),
        name="scale_embedding",
    )(member, modulation, embed_weight, embed_bias.reshape(1, -1))


def mix_kernel(left, qkv_w, qkv_b, mix, rows):
    product = dot(left[...], qkv_w[...])
    cols = product.shape[1]
    for clip in range(2):
        at = clip * 128
        high, low = split2(product[at : at + 64] + product[at + 64 : at + 128])
        mix[clip] = jnp.concatenate([high, low], axis=0)
    tail = product[256:272]
    rows[...] = jnp.concatenate(
        [tail[0:2] + tail[2:4], tail[4:6] + qkv_b[...], jnp.zeros((4, cols), f32)], axis=0
    )


def mix_weights(left, qkv_weight, qkv_bias):
    width = left.shape[1]
    cols = 256
    return pl.pallas_call(
        mix_kernel,
        grid=(qkv_weight.shape[1] // cols,),
        in_specs=[
            pl.BlockSpec(left.shape, lambda n: (0, 0)),
            pl.BlockSpec((width, cols), lambda n: (0, n)),
            pl.BlockSpec((1, cols), lambda n: (0, n)),
        ],
        out_specs=[
            pl.BlockSpec((2, 128, cols), lambda n: (0, 0, n)),
            pl.BlockSpec((8, cols), lambda n: (0, n)),
        ],
        out_shape=[
            jax.ShapeDtypeStruct((2, 128, 768), bf16),
            jax.ShapeDtypeStruct((8, 768), f32),
        ],
        compiler_params=pltpu.CompilerParams(vmem_limit_bytes=12 * MIB),
        cost_estimate=pl.CostEstimate(flops=13 * 10**8, bytes_accessed=6 * 10**6, transcendentals=0),
        name="mix_weights",
    )(left, qkv_weight, qkv_bias.reshape(1, -1))


def project(lead, own, mix, rows, gram, gvec, q_gain, k_gain, write):
    factor = math.log2(math.e) / math.sqrt(128)
    gains = q_gain[...] * factor, k_gain[...]
    count = own.shape[0]
    later = iota((count, 1), 0) // 16 % 4 >= lead
    spread = dot(own, gram[0]) + dot(own, gram[1]) + dot(own, gram[2])
    terms = (spread + gvec[0:1, :]) * own.astype(f32)
    low_lane = iota((count, 128), 1) < 64
    slope = jnp.where(later, rows[1:2, :], rows[0:1, :])
    offset = jnp.where(later, rows[3:4, :], rows[2:3, :])
    for half in range(2):
        mine = jnp.where(low_lane == (half == 0), terms, 0.0)
        variance = jnp.sum(mine, axis=1, keepdims=True) + gvec[1:2, 0:1]
        scale = lax.rsqrt(jnp.maximum(variance, 0.0) + norm_eps)
        feats = own[:, half * 64 : half * 64 + 64]
        twice = jnp.concatenate([feats, feats], axis=1)
        mixed = jnp.where(later, dot(twice, mix[1]), dot(twice, mix[0]))
        qkv = scale * (mixed + slope) + offset
        for head in range(2):
            at = head * 384
            for kind in range(2):
                part = qkv[:, at + kind * 128 : at + kind * 128 + 128]
                norm = lax.rsqrt(jnp.mean(part * part, axis=1, keepdims=True) + norm_eps)
                write(kind, head, half, (part * norm * gains[kind]).astype(bf16))
            write(2, head, half, qkv[:, at + 256 : at + 384].astype(bf16))


def attend_kernel(
    table, tokens, mix, rows, gram, gvec, q_gain, k_gain, out, parts
):
    lead = table[20]
    def write(kind, head, half, value):
        for band in range(8):
            for frame in range(4):
                at = frame * 256 + (half * 8 + band) * 16
                parts[kind, head, at : at + 16, :] = value[
                    (band * 4 + frame) * 16 : (band * 4 + frame) * 16 + 16
                ]

    own = tokens[...].reshape(512, 128)
    project(lead, own, mix, rows, gram, gvec, q_gain, k_gain, write)

    def group(begin, end):
        for head in range(2):
            key = parts[1, head, begin * 256 : end * 256, :]
            value = parts[2, head, begin * 256 : end * 256, :]
            wide = jnp.concatenate([value, jnp.ones_like(value)], axis=1)
            for frame in range(begin, end):
                score = dot(parts[0, head, frame * 256 : frame * 256 + 256, :], key, NT)
                top = jnp.max(score, axis=1, keepdims=True)
                expo = jnp.exp2(score - top)
                both = dot(expo.astype(bf16), wide)
                result = (both[:, 0:128] / both[:, 128:256]).astype(bf16)
                lanes = slice(head * 128, head * 128 + 128)
                for half in range(2):
                    for band in range(8):
                        at = (half * 8 + band) * 16
                        out[7 - band, frame, half, :, lanes] = result[at : at + 16]

    for first in (1, 2, 3):

        @pl.when(lead == first)
        def _(first=first):
            group(0, first)
            group(first, 4)


def attend(table, tokens, mix, rows, gram, gvec, q_gain, k_gain):
    smem = pl.BlockSpec(memory_space=pltpu.SMEM)
    vmem = pl.BlockSpec(memory_space=pltpu.VMEM)
    return pl.pallas_call(
        attend_kernel,
        in_specs=[smem] + [vmem] * 7,
        out_specs=vmem,
        out_shape=jax.ShapeDtypeStruct((8, 4, 2, 16, 256), bf16),
        scratch_shapes=[pltpu.VMEM((3, 2, 1024, 128), bf16)],
        compiler_params=pltpu.CompilerParams(vmem_limit_bytes=14 * MIB),
        cost_estimate=pl.CostEstimate(flops=10**9, bytes_accessed=3 * 10**6, transcendentals=1300000),
        name="attend",
    )(table, tokens, mix, rows, gram, gvec, q_gain, k_gain)


def neighbour(value, axis, step):
    count = lax.axis_size(axis)
    pairs = [(i, i + step) for i in range(count) if 0 <= i + step < count]
    return lax.ppermute(value, axis, pairs)


def swap(value, axis, mask):
    return lax.ppermute(value, axis, [(i, i ^ mask) for i in range(lax.axis_size(axis))])


def swap_pairs(value, axis, begin):
    pairs = [(i, i + 1) for i in range(begin, lax.axis_size(axis) - 1, 2)]
    return lax.ppermute(value, axis, pairs + [(b, a) for a, b in pairs])


def swap3(value, axis, unit):
    return [value] + [swap(value, axis, unit * step) for step in (3, 2, 1)][::-1]


def per_device(
    video_feat,
    clip_frames,
    clip_offset,
    conv_weight,
    conv_bias,
    latent_weight,
    latent_bias,
    embed_weight,
    embed_bias,
    modulation,
    qkv_weight,
    qkv_bias,
    q_gain,
    k_gain,
):
    seqs, heads = lax.axis_size("seq"), lax.axis_size("head")
    seq = lax.axis_index("seq")
    frames = video_feat.shape[0]
    latent_rows = latent_weight.T

    weight = conv_weight.transpose(0, 1, 2, 4, 3).reshape(27, conv_weight.shape[4], -1)
    parts = lax.all_to_all(
        fold_tap(weight, latent_rows, heads), "head", 0, 0, axis_index_groups=[list(range(heads))[::-1]]
    )
    prev = neighbour(video_feat[2:], "seq", 1)
    tap = jnp.sum(parts.astype(f32), axis=0).astype(bf16)

    count = clip_frames.shape[0]
    numbers = jnp.arange(count, dtype=jnp.int32)
    starts = jnp.sum(jnp.where(numbers[None, :] < numbers[:, None], clip_frames[None, :], 0), axis=1)
    ids = seq * frames + jnp.arange(frames, dtype=jnp.int32)
    first = jnp.max(jnp.where(starts[None, :] <= ids[:, None], starts[None, :], 0), axis=1)
    slot = seq // 2 * 2 * frames + jnp.arange(2 * frames, dtype=jnp.int32)
    inside = (clip_offset[None, :] <= slot[:, None]) & (
        slot[:, None] < (clip_offset + clip_frames)[None, :]
    )
    origin = jnp.sum(jnp.where(inside, (starts - clip_offset)[None, :] + slot[:, None], 0), axis=1)
    origin = jnp.clip(origin, 0, seqs * frames - 1)
    delays = jnp.arange(3, dtype=jnp.int32)
    source = jnp.maximum(ids[:, None] - 2 + delays[None, :], first[:, None]) - seq * frames + 2
    source = jnp.clip(source, 0, frames + 1).reshape(-1)
    leading = clip_offset == seq * frames
    lead = jnp.sum(jnp.where(leading, clip_frames, 0)).reshape(1)
    table = jnp.concatenate([source, origin, lead])
    trailing = (clip_offset > seq * frames) & (clip_offset < (seq + 1) * frames)
    member = jnp.concatenate(
        [leading[None], trailing[None], jnp.zeros((6, count), jnp.bool_)], axis=0
    ).astype(bf16)

    left, gram, gvec = scale_embedding(member, modulation, embed_weight, embed_bias)

    tap, table = lax.optimization_barrier((tap, table))
    chips = seqs // 2
    cores = [[2 * chip + core for chip in range(chips)] for core in range(2)]
    over_chips = lambda value: lax.all_to_all(value, "seq", 0, 0, axis_index_groups=cores)
    same = over_chips(jnp.broadcast_to(tap[None], (chips,) + tap.shape))
    folded = same, swap(same, "seq", 1)
    mix, rows = mix_weights(left, qkv_weight, qkv_bias)
    mixed = mix, rows, gram, gvec
    act, base = prepare(video_feat, prev, latent_rows, conv_bias, latent_bias)

    own, first, second = convolve(table, act, folded, base)
    first = swap_pairs(first, "head", 0)
    second = swap_pairs(second, "head", 1)
    pieces = finish(own, first, second, chips)
    frames_all = over_chips(pieces)
    mine, other = route(table, frames_all)
    mine, other, mixed = lax.optimization_barrier((mine, other, mixed))
    slots = mine + swap(other, "seq", 1)
    tokens = lax.all_to_all(
        jnp.broadcast_to(slots[None], (heads,) + slots.shape), "head", 0, 0, axis_index_groups=[list(range(heads))[::-1]]
    )
    gains = q_gain.reshape(1, -1), k_gain.reshape(1, -1)
    out = attend(table, tokens, *mixed, *gains)
    return out.reshape(heads * frames * 32, 256)


def solution(mesh):
    placed = (
        P("seq", "head", None, None),
        P(),
        P(),
        P(None, None, None, None, "head"),
        P(),
        P(),
        P(),
        P(),
        P(),
        P(),
        P(None, "head"),
        P("head"),
        P(),
        P(),
    )
    return jax.shard_map(
        per_device, mesh=mesh, in_specs=placed, out_specs=P("seq", "head"), check_vma=False
    )
```

```python
import functools
import math

import jax
import jax.numpy as jnp
from jax import lax
from jax.experimental import pallas as pl
from jax.experimental.pallas import tpu as pltpu
from jax.sharding import PartitionSpec as P

latent_scale = 0.476986
norm_eps = 1e-06
f32 = jnp.float32
bf16 = jnp.bfloat16
MIB = 1024 * 1024
NT = (((1,), (1,)), ((), ()))


def dot(a, b, dims=(((1,), (0,)), ((), ()))):
    return lax.dot_general(a, b, dims, preferred_element_type=f32)


def split2(value):
    high = value.astype(bf16)
    return high, (value - high.astype(f32)).astype(bf16)


def iota(shape, dim):
    return lax.broadcasted_iota(jnp.int32, shape, dim)


def fold_kernel(weight, latent, out, tap_buf, lat_buf, sems):
    band = lax.axis_index("head")
    tap = jnp.minimum(lax.axis_index("seq"), weight.shape[0] - 1)
    first = pltpu.make_async_copy(weight.at[tap], tap_buf, sems.at[0])
    second = pltpu.make_async_copy(latent, lat_buf, sems.at[1])
    first.start()
    second.start()
    second.wait()
    own = jnp.where(iota((16, 512), 1) // 64 == band, lat_buf[...].astype(f32), 0.0)
    pair = own[:, 0:128] + own[:, 128:256] + own[:, 256:384] + own[:, 384:512]
    left = (pair[:, 0:64] + pair[:, 64:128]).astype(bf16)
    first.wait()
    part = dot(left, tap_buf[...]).astype(bf16)
    for peer in range(out.shape[0]):
        out[peer] = part


def fold_tap(weight, latent_rows, copies):
    taps, outs, ins = weight.shape
    lats = latent_rows.shape[0]
    whole = pl.BlockSpec(memory_space=pl.ANY)
    return pl.pallas_call(
        fold_kernel,
        in_specs=[whole, whole],
        out_specs=pl.BlockSpec(memory_space=pltpu.VMEM),
        out_shape=jax.ShapeDtypeStruct((copies, lats, ins), bf16),
        scratch_shapes=[
            pltpu.VMEM((outs, ins), bf16),
            pltpu.VMEM((lats, ins), bf16),
            pltpu.SemaphoreType.DMA((2,)),
        ],
        compiler_params=pltpu.CompilerParams(vmem_limit_bytes=56 * MIB),
        cost_estimate=pl.CostEstimate(flops=10**6, bytes_accessed=150000, transcendentals=0),
        name="fold_tap",
    )(weight, latent_rows)


def prep_kernel(main, prev, lat, cbias, lbias, act, base):
    def silu(value):
        value = value.astype(f32)
        half = 0.5 * value
        return (half * jnp.tanh(half) + half).astype(bf16)

    for frame in range(6):
        rows = prev[frame] if frame < 2 else main[frame - 2]
        act[frame * 128 : frame * 128 + 128, :] = silu(rows.reshape(128, 512))
    weight = lat[...]
    const = jnp.sum(weight.astype(f32) * cbias[...], axis=1, keepdims=True) + lbias[...]
    for frame in range(4):
        own = main[frame].reshape(128, 512)
        base[:, frame * 128 : frame * 128 + 128] = dot(weight, own, NT) + const


def prepare(video, prev, lat, conv_bias, latent_bias):
    return pl.pallas_call(
        prep_kernel,
        out_shape=(
            jax.ShapeDtypeStruct((768, 512), bf16),
            jax.ShapeDtypeStruct((16, 512), f32),
        ),
        compiler_params=pltpu.CompilerParams(vmem_limit_bytes=8 * MIB),
        cost_estimate=pl.CostEstimate(flops=2 * 10**7, bytes_accessed=3 * 10**6, transcendentals=800000),
        name="prepare",
    )(video, prev, lat, conv_bias.reshape(1, -1), latent_bias.reshape(-1, 1))


def conv_kernel(table, act, same, other, base, own, first, second, weight, taps):
    even = lax.axis_index("head") % 2 == 0
    core = lax.axis_index("seq") % 2
    for chip in range(16):
        own_at = pl.multiple_of(chip * 32 + core * 16, 16)
        pair_at = pl.multiple_of(chip * 32 + 16 - core * 16, 16)
        weight[pl.ds(own_at, 16), :] = same[chip]
        weight[pl.ds(pair_at, 16), :] = other[chip]
    for frame in range(0, 6, 2):
        pair = dot(weight[0:432, :], act[frame * 128 : frame * 128 + 256, :], NT)
        taps[frame] = pair[:, 0:128]
        taps[frame + 1] = pair[:, 128:256]
    column = iota((16, 128), 1) % 64

    def across(parts):
        left = jnp.where(column == 0, 0.0, pltpu.roll(parts[0], 1, 1))
        right = jnp.where(column == 63, 0.0, pltpu.roll(parts[2], 127, 1))
        return parts[1] + left + right

    upper = iota((16, 128), 1) < 64
    for frame in range(4):
        total = None
        for delay in range(3):
            part = taps[table[frame * 3 + delay], delay * 144 : delay * 144 + 144, :]
            total = part if total is None else total + part
        step = [
            across([total[(a * 3 + col) * 16 : (a * 3 + col) * 16 + 16] for col in range(3)])
            for a in range(3)
        ]
        from_above = jnp.where(upper, 0.0, pltpu.roll(step[0], 64, 1))
        from_below = jnp.where(upper, pltpu.roll(step[2], 64, 1), 0.0)
        here = slice(frame * 128, frame * 128 + 128)
        own[:, here] = base[:, here] + step[1] + from_above + from_below
        half = slice(frame * 64, frame * 64 + 64)
        above, below = step[2][:, 0:64], step[0][:, 64:128]
        first[:, half] = jnp.where(even, below, above)
        second[:, half] = jnp.where(even, above, below)


def convolve(table, act, folded, base):
    smem = pl.BlockSpec(memory_space=pltpu.SMEM)
    vmem = pl.BlockSpec(memory_space=pltpu.VMEM)
    return pl.pallas_call(
        conv_kernel,
        in_specs=[smem] + [vmem] * 4,
        out_specs=(vmem, vmem, vmem),
        out_shape=(
            jax.ShapeDtypeStruct((16, 512), f32),
            jax.ShapeDtypeStruct((16, 256), f32),
            jax.ShapeDtypeStruct((16, 256), f32),
        ),
        scratch_shapes=[pltpu.VMEM((512, 512), bf16), pltpu.VMEM((6, 432, 128), f32)],
        compiler_params=pltpu.CompilerParams(vmem_limit_bytes=10 * MIB),
        cost_estimate=pl.CostEstimate(flops=4 * 10**8, bytes_accessed=2 * 10**6, transcendentals=0),
        name="convolve",
    )(table, act, *folded, base)


def finish_kernel(own, first, second, out):
    even = lax.axis_index("head") % 2 == 0
    lane = iota((16, 128), 1)
    row = iota((128, 128), 0)
    pos = iota((128, 128), 1)
    own_half = (pos % 64) // 32 == row // 64
    own_cell = (pos // 64) * 2 + pos % 2 == row % 4
    keep = own_half & own_cell
    repeat = (iota((128, 16), 0) % 64 // 4 == iota((128, 16), 1)).astype(bf16)
    pick = ((lane % 32) // 2 == iota((16, 128), 0)).astype(bf16)
    for frame in range(4):
        half = slice(frame * 64, frame * 64 + 64)
        one, two = first[:, half], second[:, half]
        edge = jnp.concatenate([jnp.where(even, two, one), jnp.where(even, one, two)], axis=1)
        latent = ((own[:, frame * 128 : frame * 128 + 128] + edge) * latent_scale).astype(bf16)
        wide = jnp.where(keep, dot(repeat, latent), 0.0).astype(bf16)
        piece = dot(pick, wide, NT).astype(bf16)
        for peer in range(out.shape[0]):
            out[peer, frame] = piece


def finish(own, first, second, copies):
    vmem = pl.BlockSpec(memory_space=pltpu.VMEM)
    return pl.pallas_call(
        finish_kernel,
        in_specs=[vmem, vmem, vmem],
        out_specs=vmem,
        out_shape=jax.ShapeDtypeStruct((copies, 4, 16, 128), bf16),
        compiler_params=pltpu.CompilerParams(vmem_limit_bytes=6 * MIB),
        cost_estimate=pl.CostEstimate(flops=10**7, bytes_accessed=10**6, transcendentals=0),
        name="finish",
    )(own, first, second)


def route_kernel(table, frames, mine, other):
    core = lax.axis_index("seq") % 2
    for out, owner in ((mine, core), (other, 1 - core)):
        for slot in range(4):
            frame = table[12 + owner * 4 + slot]
            here = (frame // 4) % 2 == core
            piece = frames[frame // 8, frame % 4]
            out[slot] = jnp.where(here, piece, jnp.zeros_like(piece))


def route(table, frames):
    smem = pl.BlockSpec(memory_space=pltpu.SMEM)
    vmem = pl.BlockSpec(memory_space=pltpu.VMEM)
    shape = jax.ShapeDtypeStruct((4, 16, 128), bf16)
    return pl.pallas_call(
        route_kernel,
        in_specs=[smem, vmem],
        out_specs=(vmem, vmem),
        out_shape=(shape, shape),
        compiler_params=pltpu.CompilerParams(vmem_limit_bytes=4 * MIB),
        cost_estimate=pl.CostEstimate(flops=1, bytes_accessed=10**6, transcendentals=0),
        name="route",
    )(table, frames)


def scale_kernel(member, modulation, embed, bias, left, gram, gvec):
    width = embed.shape[1]
    chunk = 512
    mean = jnp.sum(embed[...].astype(f32), axis=1, keepdims=True) / width
    bias_mean = jnp.sum(bias[...], axis=1, keepdims=True) / width
    whole = jnp.zeros((80, 80), f32)
    for at in range(0, width, chunk):
        here = slice(at, at + chunk)
        centred = embed[:, here].astype(f32) - mean
        cbias = bias[:, here] - bias_mean
        scale = 1.0 + dot(member[...], modulation[:, width + at : width + at + chunk])
        shift = dot(member[...], modulation[:, here])
        first, second = scale[0:1], scale[1:2]
        high, low = split2(centred * first)
        left[0:64, here] = high
        left[64:128, here] = low
        high, low = split2(centred * second)
        left[128:192, here] = high
        left[192:256, here] = low
        high, low = split2(jnp.concatenate([cbias * first, cbias * second], axis=0))
        left[256:272, here] = jnp.concatenate(
            [high.astype(f32), low.astype(f32), shift[0:2], jnp.zeros((10, chunk), f32)], axis=0
        ).astype(bf16)
        full = jnp.concatenate([centred, cbias, jnp.zeros((15, chunk), f32)], axis=0)
        high, low = split2(full)
        whole = whole + (dot(high, high, NT) + dot(high, low, NT) + dot(low, high, NT))
    whole = whole * (1.0 / width)
    square = whole[0:64, 0:64]
    blank = jnp.zeros((64, 64), f32)
    block = jnp.concatenate(
        [jnp.concatenate([square, blank], axis=1), jnp.concatenate([blank, square], axis=1)], axis=0
    )
    top = block.astype(bf16)
    rest = block - top.astype(f32)
    mid = rest.astype(bf16)
    gram[0] = top
    gram[1] = mid
    gram[2] = (rest - mid.astype(f32)).astype(bf16)
    cross = 2.0 * whole[64:65, 0:64]
    const = jnp.broadcast_to(whole[64:65, 64:65], (1, 128))
    gvec[...] = jnp.concatenate(
        [jnp.concatenate([cross, cross], axis=1), const, jnp.zeros((6, 128), f32)], axis=0
    )


def scale_embedding(member, modulation, embed_weight, embed_bias):
    width = embed_weight.shape[1]
    vmem = pl.BlockSpec(memory_space=pltpu.VMEM)
    return pl.pallas_call(
        scale_kernel,
        in_specs=[vmem] * 4,
        out_specs=[vmem] * 3,
        out_shape=[
            jax.ShapeDtypeStruct((272, width), bf16),
            jax.ShapeDtypeStruct((3, 128, 128), bf16),
            jax.ShapeDtypeStruct((8, 128), f32),
        ],
        compiler_params=pltpu.CompilerParams(vmem_limit_bytes=8 * MIB),
        cost_estimate=pl.CostEstimate(flops=10**8, bytes_accessed=3 * 10**6, transcendentals=0),
        name="scale_embedding",
    )(member, modulation, embed_weight, embed_bias.reshape(1, -1))


def mix_kernel(left, qkv_w, qkv_b, mix, rows):
    product = dot(left[...], qkv_w[...])
    cols = product.shape[1]
    for clip in range(2):
        at = clip * 128
        high, low = split2(product[at : at + 64] + product[at + 64 : at + 128])
        mix[clip] = jnp.concatenate([high, low], axis=0)
    tail = product[256:272]
    rows[...] = jnp.concatenate(
        [tail[0:2] + tail[2:4], tail[4:6] + qkv_b[...], jnp.zeros((4, cols), f32)], axis=0
    )


def mix_weights(left, qkv_weight, qkv_bias):
    width = left.shape[1]
    cols = 256
    return pl.pallas_call(
        mix_kernel,
        grid=(qkv_weight.shape[1] // cols,),
        in_specs=[
            pl.BlockSpec(left.shape, lambda n: (0, 0)),
            pl.BlockSpec((width, cols), lambda n: (0, n)),
            pl.BlockSpec((1, cols), lambda n: (0, n)),
        ],
        out_specs=[
            pl.BlockSpec((2, 128, cols), lambda n: (0, 0, n)),
            pl.BlockSpec((8, cols), lambda n: (0, n)),
        ],
        out_shape=[
            jax.ShapeDtypeStruct((2, 128, 768), bf16),
            jax.ShapeDtypeStruct((8, 768), f32),
        ],
        compiler_params=pltpu.CompilerParams(vmem_limit_bytes=12 * MIB),
        cost_estimate=pl.CostEstimate(flops=13 * 10**8, bytes_accessed=6 * 10**6, transcendentals=0),
        name="mix_weights",
    )(left, qkv_weight, qkv_bias.reshape(1, -1))


def project(lead, own, mix, rows, gram, gvec, q_gain, k_gain, write):
    factor = math.log2(math.e) / math.sqrt(128)
    gain = q_gain[...] * k_gain[...] * factor
    count = own.shape[0]
    later = iota((count, 1), 0) // 16 % 4 >= lead
    spread = dot(own, gram[0]) + dot(own, gram[1]) + dot(own, gram[2])
    terms = (spread + gvec[0:1, :]) * own.astype(f32)
    low_lane = iota((count, 128), 1) < 64
    slope = jnp.where(later, rows[1:2, :], rows[0:1, :])
    offset = jnp.where(later, rows[3:4, :], rows[2:3, :])
    for half in range(2):
        mine = jnp.where(low_lane == (half == 0), terms, 0.0)
        variance = jnp.sum(mine, axis=1, keepdims=True) + gvec[1:2, 0:1]
        scale = lax.rsqrt(jnp.maximum(variance, 0.0) + norm_eps)
        feats = own[:, half * 64 : half * 64 + 64]
        twice = jnp.concatenate([feats, feats], axis=1)
        mixed = jnp.where(later, dot(twice, mix[1]), dot(twice, mix[0]))
        qkv = scale * (mixed + slope) + offset
        for head in range(2):
            at = head * 384
            for kind in range(2):
                part = qkv[:, at + kind * 128 : at + kind * 128 + 128]
                norm = lax.rsqrt(jnp.mean(part * part, axis=1, keepdims=True) + norm_eps)
                part = part * norm
                write(kind, head, half, (part * gain if kind == 0 else part).astype(bf16))
            write(2, head, half, qkv[:, at + 256 : at + 384].astype(bf16))


def attend_kernel(
    table, tokens, mix, rows, gram, gvec, q_gain, k_gain, out, parts
):
    lead = table[20]
    def write(kind, head, half, value):
        for band in range(8):
            for frame in range(4):
                at = frame * 256 + (half * 8 + band) * 16
                parts[kind, head, at : at + 16, :] = value[
                    (band * 4 + frame) * 16 : (band * 4 + frame) * 16 + 16
                ]

    own = tokens[...].reshape(512, 128)
    project(lead, own, mix, rows, gram, gvec, q_gain, k_gain, write)

    def group(begin, end):
        for head in range(2):
            key = parts[1, head, begin * 256 : end * 256, :]
            value = parts[2, head, begin * 256 : end * 256, :]
            wide = jnp.concatenate([value, jnp.ones_like(value)], axis=1)
            for frame in range(begin, end):
                score = dot(parts[0, head, frame * 256 : frame * 256 + 256, :], key, NT)
                top = jnp.max(score, axis=1, keepdims=True)
                expo = jnp.exp2(score - top)
                both = dot(expo.astype(bf16), wide)
                result = (both[:, 0:128] / both[:, 128:256]).astype(bf16)
                lanes = slice(head * 128, head * 128 + 128)
                for half in range(2):
                    for band in range(8):
                        at = (half * 8 + band) * 16
                        out[7 - band, frame, half, :, lanes] = result[at : at + 16]

    for first in (1, 2, 3):

        @pl.when(lead == first)
        def _(first=first):
            group(0, first)
            group(first, 4)


def attend(table, tokens, mix, rows, gram, gvec, q_gain, k_gain):
    smem = pl.BlockSpec(memory_space=pltpu.SMEM)
    vmem = pl.BlockSpec(memory_space=pltpu.VMEM)
    return pl.pallas_call(
        attend_kernel,
        in_specs=[smem] + [vmem] * 7,
        out_specs=vmem,
        out_shape=jax.ShapeDtypeStruct((8, 4, 2, 16, 256), bf16),
        scratch_shapes=[pltpu.VMEM((3, 2, 1024, 128), bf16)],
        compiler_params=pltpu.CompilerParams(vmem_limit_bytes=14 * MIB),
        cost_estimate=pl.CostEstimate(flops=10**9, bytes_accessed=3 * 10**6, transcendentals=1300000),
        name="attend",
    )(table, tokens, mix, rows, gram, gvec, q_gain, k_gain)


def neighbour(value, axis, step):
    count = lax.axis_size(axis)
    pairs = [(i, i + step) for i in range(count) if 0 <= i + step < count]
    return lax.ppermute(value, axis, pairs)


def swap(value, axis, mask):
    return lax.ppermute(value, axis, [(i, i ^ mask) for i in range(lax.axis_size(axis))])


def swap_pairs(value, axis, begin):
    pairs = [(i, i + 1) for i in range(begin, lax.axis_size(axis) - 1, 2)]
    return lax.ppermute(value, axis, pairs + [(b, a) for a, b in pairs])


def swap3(value, axis, unit):
    return [value] + [swap(value, axis, unit * step) for step in (3, 2, 1)][::-1]


def per_device(
    video_feat,
    clip_frames,
    clip_offset,
    conv_weight,
    conv_bias,
    latent_weight,
    latent_bias,
    embed_weight,
    embed_bias,
    modulation,
    qkv_weight,
    qkv_bias,
    q_gain,
    k_gain,
):
    seqs, heads = lax.axis_size("seq"), lax.axis_size("head")
    seq = lax.axis_index("seq")
    frames = video_feat.shape[0]
    latent_rows = latent_weight.T

    weight = conv_weight.transpose(0, 1, 2, 4, 3).reshape(27, conv_weight.shape[4], -1)
    parts = lax.all_to_all(
        fold_tap(weight, latent_rows, heads), "head", 0, 0, axis_index_groups=[list(range(heads))[::-1]]
    )
    prev = neighbour(video_feat[2:], "seq", 1)
    tap = jnp.sum(parts.astype(f32), axis=0).astype(bf16)

    count = clip_frames.shape[0]
    numbers = jnp.arange(count, dtype=jnp.int32)
    starts = jnp.sum(jnp.where(numbers[None, :] < numbers[:, None], clip_frames[None, :], 0), axis=1)
    ids = seq * frames + jnp.arange(frames, dtype=jnp.int32)
    first = jnp.max(jnp.where(starts[None, :] <= ids[:, None], starts[None, :], 0), axis=1)
    slot = seq // 2 * 2 * frames + jnp.arange(2 * frames, dtype=jnp.int32)
    inside = (clip_offset[None, :] <= slot[:, None]) & (
        slot[:, None] < (clip_offset + clip_frames)[None, :]
    )
    origin = jnp.sum(jnp.where(inside, (starts - clip_offset)[None, :] + slot[:, None], 0), axis=1)
    origin = jnp.clip(origin, 0, seqs * frames - 1)
    delays = jnp.arange(3, dtype=jnp.int32)
    source = jnp.maximum(ids[:, None] - 2 + delays[None, :], first[:, None]) - seq * frames + 2
    source = jnp.clip(source, 0, frames + 1).reshape(-1)
    leading = clip_offset == seq * frames
    lead = jnp.sum(jnp.where(leading, clip_frames, 0)).reshape(1)
    table = jnp.concatenate([source, origin, lead])
    trailing = (clip_offset > seq * frames) & (clip_offset < (seq + 1) * frames)
    member = jnp.concatenate(
        [leading[None], trailing[None], jnp.zeros((6, count), jnp.bool_)], axis=0
    ).astype(bf16)

    left, gram, gvec = scale_embedding(member, modulation, embed_weight, embed_bias)

    tap, table = lax.optimization_barrier((tap, table))
    chips = seqs // 2
    cores = [[2 * chip + core for chip in range(chips)] for core in range(2)]
    over_chips = lambda value: lax.all_to_all(value, "seq", 0, 0, axis_index_groups=cores)
    same = over_chips(jnp.broadcast_to(tap[None], (chips,) + tap.shape))
    mix, rows = mix_weights(left, qkv_weight, qkv_bias)
    mixed = mix, rows, gram, gvec
    same, mixed = lax.optimization_barrier((same, mixed))
    folded = same, swap(same, "seq", 1)
    act, base = prepare(video_feat, prev, latent_rows, conv_bias, latent_bias)

    own, first, second = convolve(table, act, folded, base)
    first = swap_pairs(first, "head", 0)
    second = swap_pairs(second, "head", 1)
    pieces = finish(own, first, second, chips)
    frames_all = over_chips(pieces)
    mine, other = route(table, frames_all)
    slots = mine + swap(other, "seq", 1)
    tokens = lax.all_to_all(
        jnp.broadcast_to(slots[None], (heads,) + slots.shape), "head", 0, 0, axis_index_groups=[list(range(heads))[::-1]]
    )
    gains = q_gain.reshape(1, -1), k_gain.reshape(1, -1)
    out = attend(table, tokens, *mixed, *gains)
    return out.reshape(heads * frames * 32, 256)


def solution(mesh):
    placed = (
        P("seq", "head", None, None),
        P(),
        P(),
        P(None, None, None, None, "head"),
        P(),
        P(),
        P(),
        P(),
        P(),
        P(),
        P(None, "head"),
        P("head"),
        P(),
        P(),
    )
    return jax.shard_map(
        per_device, mesh=mesh, in_specs=placed, out_specs=P("seq", "head"), check_vma=False
    )
```

```python
import functools
import math

import jax
import jax.numpy as jnp
from jax import lax
from jax.experimental import pallas as pl
from jax.experimental.pallas import tpu as pltpu
from jax.sharding import PartitionSpec as P

latent_scale = 0.476986
norm_eps = 1e-06
f32 = jnp.float32
bf16 = jnp.bfloat16
MIB = 1024 * 1024
NT = (((1,), (1,)), ((), ()))


def dot(a, b, dims=(((1,), (0,)), ((), ()))):
    return lax.dot_general(a, b, dims, preferred_element_type=f32)


def split2(value):
    high = value.astype(bf16)
    return high, (value - high.astype(f32)).astype(bf16)


def iota(shape, dim):
    return lax.broadcasted_iota(jnp.int32, shape, dim)


def fold_kernel(weight, latent, out, tap_buf, lat_buf, sems):
    band = lax.axis_index("head")
    tap = jnp.minimum(lax.axis_index("seq"), weight.shape[0] - 1)
    first = pltpu.make_async_copy(weight.at[tap], tap_buf, sems.at[0])
    second = pltpu.make_async_copy(latent, lat_buf, sems.at[1])
    first.start()
    second.start()
    second.wait()
    own = jnp.where(iota((16, 512), 1) // 64 == band, lat_buf[...].astype(f32), 0.0)
    pair = own[:, 0:128] + own[:, 128:256] + own[:, 256:384] + own[:, 384:512]
    left = (pair[:, 0:64] + pair[:, 64:128]).astype(bf16)
    first.wait()
    part = dot(left, tap_buf[...]).astype(bf16)
    for peer in range(out.shape[0]):
        out[peer] = part


def fold_tap(weight, latent_rows, copies):
    taps, outs, ins = weight.shape
    lats = latent_rows.shape[0]
    whole = pl.BlockSpec(memory_space=pl.ANY)
    return pl.pallas_call(
        fold_kernel,
        in_specs=[whole, whole],
        out_specs=pl.BlockSpec(memory_space=pltpu.VMEM),
        out_shape=jax.ShapeDtypeStruct((copies, lats, ins), bf16),
        scratch_shapes=[
            pltpu.VMEM((outs, ins), bf16),
            pltpu.VMEM((lats, ins), bf16),
            pltpu.SemaphoreType.DMA((2,)),
        ],
        compiler_params=pltpu.CompilerParams(vmem_limit_bytes=56 * MIB),
        cost_estimate=pl.CostEstimate(flops=10**6, bytes_accessed=150000, transcendentals=0),
        name="fold_tap",
    )(weight, latent_rows)


def prep_kernel(main, prev, lat, cbias, lbias, act, base):
    def silu(value):
        value = value.astype(f32)
        half = 0.5 * value
        return (half * jnp.tanh(half) + half).astype(bf16)

    for frame in range(6):
        rows = prev[frame] if frame < 2 else main[frame - 2]
        act[frame * 128 : frame * 128 + 128, :] = silu(rows.reshape(128, 512))
    weight = lat[...]
    const = jnp.sum(weight.astype(f32) * cbias[...], axis=1, keepdims=True) + lbias[...]
    for frame in range(4):
        own = main[frame].reshape(128, 512)
        base[:, frame * 128 : frame * 128 + 128] = dot(weight, own, NT) + const


def prepare(video, prev, lat, conv_bias, latent_bias):
    return pl.pallas_call(
        prep_kernel,
        out_shape=(
            jax.ShapeDtypeStruct((768, 512), bf16),
            jax.ShapeDtypeStruct((16, 512), f32),
        ),
        compiler_params=pltpu.CompilerParams(vmem_limit_bytes=8 * MIB),
        cost_estimate=pl.CostEstimate(flops=2 * 10**7, bytes_accessed=3 * 10**6, transcendentals=800000),
        name="prepare",
    )(video, prev, lat, conv_bias.reshape(1, -1), latent_bias.reshape(-1, 1))


def conv_kernel(table, act, same, other, base, own, first, second, weight, taps):
    even = lax.axis_index("head") % 2 == 0
    core = lax.axis_index("seq") % 2
    for chip in range(16):
        own_at = pl.multiple_of(chip * 32 + core * 16, 16)
        pair_at = pl.multiple_of(chip * 32 + 16 - core * 16, 16)
        weight[pl.ds(own_at, 16), :] = same[chip]
        weight[pl.ds(pair_at, 16), :] = other[chip]
    for frame in range(0, 6, 2):
        pair = dot(weight[0:432, :], act[frame * 128 : frame * 128 + 256, :], NT)
        taps[frame] = pair[:, 0:128]
        taps[frame + 1] = pair[:, 128:256]
    column = iota((16, 128), 1) % 64

    def across(parts):
        left = jnp.where(column == 0, 0.0, pltpu.roll(parts[0], 1, 1))
        right = jnp.where(column == 63, 0.0, pltpu.roll(parts[2], 127, 1))
        return parts[1] + left + right

    upper = iota((16, 128), 1) < 64
    for frame in range(4):
        total = None
        for delay in range(3):
            part = taps[table[frame * 3 + delay], delay * 144 : delay * 144 + 144, :]
            total = part if total is None else total + part
        step = [
            across([total[(a * 3 + col) * 16 : (a * 3 + col) * 16 + 16] for col in range(3)])
            for a in range(3)
        ]
        from_above = jnp.where(upper, 0.0, pltpu.roll(step[0], 64, 1))
        from_below = jnp.where(upper, pltpu.roll(step[2], 64, 1), 0.0)
        here = slice(frame * 128, frame * 128 + 128)
        own[:, here] = base[:, here] + step[1] + from_above + from_below
        half = slice(frame * 64, frame * 64 + 64)
        above, below = step[2][:, 0:64], step[0][:, 64:128]
        first[:, half] = jnp.where(even, below, above)
        second[:, half] = jnp.where(even, above, below)


def convolve(table, act, folded, base):
    smem = pl.BlockSpec(memory_space=pltpu.SMEM)
    vmem = pl.BlockSpec(memory_space=pltpu.VMEM)
    return pl.pallas_call(
        conv_kernel,
        in_specs=[smem] + [vmem] * 4,
        out_specs=(vmem, vmem, vmem),
        out_shape=(
            jax.ShapeDtypeStruct((16, 512), f32),
            jax.ShapeDtypeStruct((16, 256), f32),
            jax.ShapeDtypeStruct((16, 256), f32),
        ),
        scratch_shapes=[pltpu.VMEM((512, 512), bf16), pltpu.VMEM((6, 432, 128), f32)],
        compiler_params=pltpu.CompilerParams(vmem_limit_bytes=10 * MIB),
        cost_estimate=pl.CostEstimate(flops=4 * 10**8, bytes_accessed=2 * 10**6, transcendentals=0),
        name="convolve",
    )(table, act, *folded, base)


def finish_kernel(own, first, second, out):
    even = lax.axis_index("head") % 2 == 0
    lane = iota((16, 128), 1)
    row = iota((128, 128), 0)
    pos = iota((128, 128), 1)
    own_half = (pos % 64) // 32 == row // 64
    own_cell = (pos // 64) * 2 + pos % 2 == row % 4
    keep = own_half & own_cell
    repeat = (iota((128, 16), 0) % 64 // 4 == iota((128, 16), 1)).astype(bf16)
    pick = ((lane % 32) // 2 == iota((16, 128), 0)).astype(bf16)
    for frame in range(4):
        half = slice(frame * 64, frame * 64 + 64)
        one, two = first[:, half], second[:, half]
        edge = jnp.concatenate([jnp.where(even, two, one), jnp.where(even, one, two)], axis=1)
        latent = ((own[:, frame * 128 : frame * 128 + 128] + edge) * latent_scale).astype(bf16)
        wide = jnp.where(keep, dot(repeat, latent), 0.0).astype(bf16)
        piece = dot(pick, wide, NT).astype(bf16)
        for peer in range(out.shape[0]):
            out[peer, frame] = piece


def finish(own, first, second, copies):
    vmem = pl.BlockSpec(memory_space=pltpu.VMEM)
    return pl.pallas_call(
        finish_kernel,
        in_specs=[vmem, vmem, vmem],
        out_specs=vmem,
        out_shape=jax.ShapeDtypeStruct((copies, 4, 16, 128), bf16),
        compiler_params=pltpu.CompilerParams(vmem_limit_bytes=6 * MIB),
        cost_estimate=pl.CostEstimate(flops=10**7, bytes_accessed=10**6, transcendentals=0),
        name="finish",
    )(own, first, second)


def route_kernel(table, frames, mine, other):
    core = lax.axis_index("seq") % 2
    for out, owner in ((mine, core), (other, 1 - core)):
        for slot in range(4):
            frame = table[12 + owner * 4 + slot]
            here = (frame // 4) % 2 == core
            piece = frames[frame // 8, frame % 4]
            out[slot] = jnp.where(here, piece, jnp.zeros_like(piece))


def route(table, frames):
    smem = pl.BlockSpec(memory_space=pltpu.SMEM)
    vmem = pl.BlockSpec(memory_space=pltpu.VMEM)
    shape = jax.ShapeDtypeStruct((4, 16, 128), bf16)
    return pl.pallas_call(
        route_kernel,
        in_specs=[smem, vmem],
        out_specs=(vmem, vmem),
        out_shape=(shape, shape),
        compiler_params=pltpu.CompilerParams(vmem_limit_bytes=4 * MIB),
        cost_estimate=pl.CostEstimate(flops=1, bytes_accessed=10**6, transcendentals=0),
        name="route",
    )(table, frames)


def scale_kernel(member, modulation, embed, bias, left, gram, gvec):
    width = embed.shape[1]
    chunk = 512
    mean = jnp.sum(embed[...].astype(f32), axis=1, keepdims=True) / width
    bias_mean = jnp.sum(bias[...], axis=1, keepdims=True) / width
    whole = jnp.zeros((80, 80), f32)
    for at in range(0, width, chunk):
        here = slice(at, at + chunk)
        centred = embed[:, here].astype(f32) - mean
        cbias = bias[:, here] - bias_mean
        scale = 1.0 + dot(member[...], modulation[:, width + at : width + at + chunk])
        shift = dot(member[...], modulation[:, here])
        first, second = scale[0:1], scale[1:2]
        high, low = split2(centred * first)
        left[0:64, here] = high
        left[64:128, here] = low
        high, low = split2(centred * second)
        left[128:192, here] = high
        left[192:256, here] = low
        high, low = split2(jnp.concatenate([cbias * first, cbias * second], axis=0))
        left[256:272, here] = jnp.concatenate(
            [high.astype(f32), low.astype(f32), shift[0:2], jnp.zeros((10, chunk), f32)], axis=0
        ).astype(bf16)
        full = jnp.concatenate([centred, cbias, jnp.zeros((15, chunk), f32)], axis=0)
        high, low = split2(full)
        whole = whole + (dot(high, high, NT) + dot(high, low, NT) + dot(low, high, NT))
    whole = whole * (1.0 / width)
    square = whole[0:64, 0:64]
    blank = jnp.zeros((64, 64), f32)
    block = jnp.concatenate(
        [jnp.concatenate([square, blank], axis=1), jnp.concatenate([blank, square], axis=1)], axis=0
    )
    top = block.astype(bf16)
    rest = block - top.astype(f32)
    mid = rest.astype(bf16)
    gram[0] = top
    gram[1] = mid
    gram[2] = (rest - mid.astype(f32)).astype(bf16)
    cross = 2.0 * whole[64:65, 0:64]
    const = jnp.broadcast_to(whole[64:65, 64:65], (1, 128))
    gvec[...] = jnp.concatenate(
        [jnp.concatenate([cross, cross], axis=1), const, jnp.zeros((6, 128), f32)], axis=0
    )


def scale_embedding(member, modulation, embed_weight, embed_bias):
    width = embed_weight.shape[1]
    vmem = pl.BlockSpec(memory_space=pltpu.VMEM)
    return pl.pallas_call(
        scale_kernel,
        in_specs=[vmem] * 4,
        out_specs=[vmem] * 3,
        out_shape=[
            jax.ShapeDtypeStruct((272, width), bf16),
            jax.ShapeDtypeStruct((3, 128, 128), bf16),
            jax.ShapeDtypeStruct((8, 128), f32),
        ],
        compiler_params=pltpu.CompilerParams(vmem_limit_bytes=8 * MIB),
        cost_estimate=pl.CostEstimate(flops=10**8, bytes_accessed=3 * 10**6, transcendentals=0),
        name="scale_embedding",
    )(member, modulation, embed_weight, embed_bias.reshape(1, -1))


def mix_kernel(left, qkv_w, qkv_b, mix, rows):
    product = dot(left[...], qkv_w[...])
    cols = product.shape[1]
    for clip in range(2):
        at = clip * 128
        high, low = split2(product[at : at + 64] + product[at + 64 : at + 128])
        mix[clip] = jnp.concatenate([high, low], axis=0)
    tail = product[256:272]
    rows[...] = jnp.concatenate(
        [tail[0:2] + tail[2:4], tail[4:6] + qkv_b[...], jnp.zeros((4, cols), f32)], axis=0
    )


def mix_weights(left, qkv_weight, qkv_bias):
    width = left.shape[1]
    cols = 256
    return pl.pallas_call(
        mix_kernel,
        grid=(qkv_weight.shape[1] // cols,),
        in_specs=[
            pl.BlockSpec(left.shape, lambda n: (0, 0)),
            pl.BlockSpec((width, cols), lambda n: (0, n)),
            pl.BlockSpec((1, cols), lambda n: (0, n)),
        ],
        out_specs=[
            pl.BlockSpec((2, 128, cols), lambda n: (0, 0, n)),
            pl.BlockSpec((8, cols), lambda n: (0, n)),
        ],
        out_shape=[
            jax.ShapeDtypeStruct((2, 128, 768), bf16),
            jax.ShapeDtypeStruct((8, 768), f32),
        ],
        compiler_params=pltpu.CompilerParams(vmem_limit_bytes=12 * MIB),
        cost_estimate=pl.CostEstimate(flops=13 * 10**8, bytes_accessed=6 * 10**6, transcendentals=0),
        name="mix_weights",
    )(left, qkv_weight, qkv_bias.reshape(1, -1))


def project(clip, begin, end, tokens, mix, rows, gram, gvec, q_gain, k_gain, parts):
    factor = math.log2(math.e) / math.sqrt(128)
    gain = q_gain[...] * k_gain[...] * factor
    own = jnp.concatenate([tokens[:, frame].reshape(128, 128) for frame in range(begin, end)], axis=0)
    spread = dot(own, gram[0]) + dot(own, gram[1]) + dot(own, gram[2])
    terms = (spread + gvec[0:1, :]) * own.astype(f32)
    low_lane = iota(own.shape, 1) < 64
    for half in range(2):
        mine = jnp.where(low_lane == (half == 0), terms, 0.0)
        variance = jnp.sum(mine, axis=1, keepdims=True) + gvec[1:2, 0:1]
        scale = lax.rsqrt(jnp.maximum(variance, 0.0) + norm_eps)
        feats = own[:, half * 64 : half * 64 + 64]
        twice = jnp.concatenate([feats, feats], axis=1)
        qkv = scale * (dot(twice, mix[clip]) + rows[clip : clip + 1, :]) + rows[clip + 2 : clip + 3, :]
        for head in range(2):
            at = head * 384
            for kind in range(3):
                part = qkv[:, at + kind * 128 : at + kind * 128 + 128]
                if kind < 2:
                    part = part * lax.rsqrt(jnp.mean(part * part, axis=1, keepdims=True) + norm_eps)
                if kind == 0:
                    part = part * gain
                part = part.astype(bf16)
                for frame in range(begin, end):
                    place = frame * 256 + half * 128
                    parts[kind, head, place : place + 128, :] = part[
                        (frame - begin) * 128 : (frame - begin) * 128 + 128
                    ]


def attend_kernel(
    table, tokens, mix, rows, gram, gvec, q_gain, k_gain, out, parts
):
    lead = table[20]
    shared = (tokens, mix, rows, gram, gvec, q_gain, k_gain, parts)

    def group(begin, end):
        for head in range(2):
            key = parts[1, head, begin * 256 : end * 256, :]
            value = parts[2, head, begin * 256 : end * 256, :]
            wide = jnp.concatenate([value, jnp.ones_like(value)], axis=1)
            for frame in range(begin, end):
                score = dot(parts[0, head, frame * 256 : frame * 256 + 256, :], key, NT)
                top = jnp.max(score, axis=1, keepdims=True)
                expo = jnp.exp2(score - top)
                both = dot(expo.astype(bf16), wide)
                result = (both[:, 0:128] / both[:, 128:256]).astype(bf16)
                lanes = slice(head * 128, head * 128 + 128)
                for half in range(2):
                    for band in range(8):
                        at = (half * 8 + band) * 16
                        out[7 - band, frame, half, :, lanes] = result[at : at + 16]

    for first in (1, 2, 3):

        @pl.when(lead == first)
        def _(first=first):
            project(0, 0, first, *shared)
            project(1, first, 4, *shared)
            group(0, first)
            group(first, 4)


def attend(table, tokens, mix, rows, gram, gvec, q_gain, k_gain):
    smem = pl.BlockSpec(memory_space=pltpu.SMEM)
    vmem = pl.BlockSpec(memory_space=pltpu.VMEM)
    return pl.pallas_call(
        attend_kernel,
        in_specs=[smem] + [vmem] * 7,
        out_specs=vmem,
        out_shape=jax.ShapeDtypeStruct((8, 4, 2, 16, 256), bf16),
        scratch_shapes=[pltpu.VMEM((3, 2, 1024, 128), bf16)],
        compiler_params=pltpu.CompilerParams(vmem_limit_bytes=14 * MIB),
        cost_estimate=pl.CostEstimate(flops=10**9, bytes_accessed=3 * 10**6, transcendentals=1300000),
        name="attend",
    )(table, tokens, mix, rows, gram, gvec, q_gain, k_gain)


def neighbour(value, axis, step):
    count = lax.axis_size(axis)
    pairs = [(i, i + step) for i in range(count) if 0 <= i + step < count]
    return lax.ppermute(value, axis, pairs)


def swap(value, axis, mask):
    return lax.ppermute(value, axis, [(i, i ^ mask) for i in range(lax.axis_size(axis))])


def swap_pairs(value, axis, begin):
    pairs = [(i, i + 1) for i in range(begin, lax.axis_size(axis) - 1, 2)]
    return lax.ppermute(value, axis, pairs + [(b, a) for a, b in pairs])


def swap3(value, axis, unit):
    return [value] + [swap(value, axis, unit * step) for step in (3, 2, 1)][::-1]


def per_device(
    video_feat,
    clip_frames,
    clip_offset,
    conv_weight,
    conv_bias,
    latent_weight,
    latent_bias,
    embed_weight,
    embed_bias,
    modulation,
    qkv_weight,
    qkv_bias,
    q_gain,
    k_gain,
):
    seqs, heads = lax.axis_size("seq"), lax.axis_size("head")
    seq = lax.axis_index("seq")
    frames = video_feat.shape[0]
    latent_rows = latent_weight.T

    weight = conv_weight.transpose(0, 1, 2, 4, 3).reshape(27, conv_weight.shape[4], -1)
    parts = lax.all_to_all(
        fold_tap(weight, latent_rows, heads), "head", 0, 0, axis_index_groups=[list(range(heads))[::-1]]
    )
    prev = neighbour(video_feat[2:], "seq", 1)
    tap = jnp.sum(parts.astype(f32), axis=0).astype(bf16)

    count = clip_frames.shape[0]
    numbers = jnp.arange(count, dtype=jnp.int32)
    starts = jnp.sum(jnp.where(numbers[None, :] < numbers[:, None], clip_frames[None, :], 0), axis=1)
    ids = seq * frames + jnp.arange(frames, dtype=jnp.int32)
    first = jnp.max(jnp.where(starts[None, :] <= ids[:, None], starts[None, :], 0), axis=1)
    slot = seq // 2 * 2 * frames + jnp.arange(2 * frames, dtype=jnp.int32)
    inside = (clip_offset[None, :] <= slot[:, None]) & (
        slot[:, None] < (clip_offset + clip_frames)[None, :]
    )
    origin = jnp.sum(jnp.where(inside, (starts - clip_offset)[None, :] + slot[:, None], 0), axis=1)
    origin = jnp.clip(origin, 0, seqs * frames - 1)
    delays = jnp.arange(3, dtype=jnp.int32)
    source = jnp.maximum(ids[:, None] - 2 + delays[None, :], first[:, None]) - seq * frames + 2
    source = jnp.clip(source, 0, frames + 1).reshape(-1)
    leading = clip_offset == seq * frames
    lead = jnp.sum(jnp.where(leading, clip_frames, 0)).reshape(1)
    table = jnp.concatenate([source, origin, lead])
    trailing = (clip_offset > seq * frames) & (clip_offset < (seq + 1) * frames)
    member = jnp.concatenate(
        [leading[None], trailing[None], jnp.zeros((6, count), jnp.bool_)], axis=0
    ).astype(bf16)

    left, gram, gvec = scale_embedding(member, modulation, embed_weight, embed_bias)

    tap, table = lax.optimization_barrier((tap, table))
    chips = seqs // 2
    cores = [[2 * chip + core for chip in range(chips)] for core in range(2)]
    over_chips = lambda value: lax.all_to_all(value, "seq", 0, 0, axis_index_groups=cores)
    same = over_chips(jnp.broadcast_to(tap[None], (chips,) + tap.shape))
    mix, rows = mix_weights(left, qkv_weight, qkv_bias)
    mixed = mix, rows, gram, gvec
    same, mixed = lax.optimization_barrier((same, mixed))
    folded = same, swap(same, "seq", 1)
    act, base = prepare(video_feat, prev, latent_rows, conv_bias, latent_bias)

    own, first, second = convolve(table, act, folded, base)
    first = swap_pairs(first, "head", 0)
    second = swap_pairs(second, "head", 1)
    pieces = finish(own, first, second, chips)
    frames_all = over_chips(pieces)
    mine, other = route(table, frames_all)
    slots = mine + swap(other, "seq", 1)
    tokens = lax.all_to_all(
        jnp.broadcast_to(slots[None], (heads,) + slots.shape), "head", 0, 0, axis_index_groups=[list(range(heads))[::-1]]
    )
    gains = q_gain.reshape(1, -1), k_gain.reshape(1, -1)
    out = attend(table, tokens, *mixed, *gains)
    return out.reshape(heads * frames * 32, 256)


def solution(mesh):
    placed = (
        P("seq", "head", None, None),
        P(),
        P(),
        P(None, None, None, None, "head"),
        P(),
        P(),
        P(),
        P(),
        P(),
        P(),
        P(None, "head"),
        P("head"),
        P(),
        P(),
    )
    return jax.shard_map(
        per_device, mesh=mesh, in_specs=placed, out_specs=P("seq", "head"), check_vma=False
    )
```

```python
import functools
import math

import jax
import jax.numpy as jnp
from jax import lax
from jax.experimental import pallas as pl
from jax.experimental.pallas import tpu as pltpu
from jax.sharding import PartitionSpec as P

latent_scale = 0.476986
norm_eps = 1e-06
f32 = jnp.float32
bf16 = jnp.bfloat16
MIB = 1024 * 1024
NT = (((1,), (1,)), ((), ()))


def dot(a, b, dims=(((1,), (0,)), ((), ()))):
    return lax.dot_general(a, b, dims, preferred_element_type=f32)


def split2(value):
    high = value.astype(bf16)
    return high, (value - high.astype(f32)).astype(bf16)


def iota(shape, dim):
    return lax.broadcasted_iota(jnp.int32, shape, dim)


def fold_kernel(weight, latent, out, tap_buf, lat_buf, sems):
    band = lax.axis_index("head")
    tap = jnp.minimum(lax.axis_index("seq"), weight.shape[0] - 1)
    first = pltpu.make_async_copy(weight.at[tap], tap_buf, sems.at[0])
    second = pltpu.make_async_copy(latent, lat_buf, sems.at[1])
    first.start()
    second.start()
    second.wait()
    own = jnp.where(iota((16, 512), 1) // 64 == band, lat_buf[...].astype(f32), 0.0)
    pair = own[:, 0:128] + own[:, 128:256] + own[:, 256:384] + own[:, 384:512]
    left = (pair[:, 0:64] + pair[:, 64:128]).astype(bf16)
    first.wait()
    part = dot(left, tap_buf[...]).astype(bf16)
    for peer in range(out.shape[0]):
        out[peer] = part


def fold_tap(weight, latent_rows, copies):
    taps, outs, ins = weight.shape
    lats = latent_rows.shape[0]
    whole = pl.BlockSpec(memory_space=pl.ANY)
    return pl.pallas_call(
        fold_kernel,
        in_specs=[whole, whole],
        out_specs=pl.BlockSpec(memory_space=pltpu.VMEM),
        out_shape=jax.ShapeDtypeStruct((copies, lats, ins), bf16),
        scratch_shapes=[
            pltpu.VMEM((outs, ins), bf16),
            pltpu.VMEM((lats, ins), bf16),
            pltpu.SemaphoreType.DMA((2,)),
        ],
        compiler_params=pltpu.CompilerParams(vmem_limit_bytes=56 * MIB),
        cost_estimate=pl.CostEstimate(flops=10**6, bytes_accessed=150000, transcendentals=0),
        name="fold_tap",
    )(weight, latent_rows)


def prep_kernel(main, prev, lat, cbias, lbias, act, base):
    def silu(value):
        value = value.astype(f32)
        half = 0.5 * value
        return (half * jnp.tanh(half) + half).astype(bf16)

    for frame in range(6):
        rows = prev[frame] if frame < 2 else main[frame - 2]
        act[frame * 128 : frame * 128 + 128, :] = silu(rows.reshape(128, 512))
    weight = lat[...]
    const = jnp.sum(weight.astype(f32) * cbias[...], axis=1, keepdims=True) + lbias[...]
    for frame in range(4):
        own = main[frame].reshape(128, 512)
        base[:, frame * 128 : frame * 128 + 128] = dot(weight, own, NT) + const


def prepare(video, prev, lat, conv_bias, latent_bias):
    return pl.pallas_call(
        prep_kernel,
        out_shape=(
            jax.ShapeDtypeStruct((768, 512), bf16),
            jax.ShapeDtypeStruct((16, 512), f32),
        ),
        compiler_params=pltpu.CompilerParams(vmem_limit_bytes=8 * MIB),
        cost_estimate=pl.CostEstimate(flops=2 * 10**7, bytes_accessed=3 * 10**6, transcendentals=800000),
        name="prepare",
    )(video, prev, lat, conv_bias.reshape(1, -1), latent_bias.reshape(-1, 1))


def conv_kernel(table, act, same, other, base, own, first, second, weight, taps):
    even = lax.axis_index("head") % 2 == 0
    core = lax.axis_index("seq") % 2
    for chip in range(16):
        own_at = pl.multiple_of(chip * 32 + core * 16, 16)
        pair_at = pl.multiple_of(chip * 32 + 16 - core * 16, 16)
        weight[pl.ds(own_at, 16), :] = same[chip]
        weight[pl.ds(pair_at, 16), :] = other[chip]
    for frame in range(0, 6, 2):
        pair = dot(weight[0:432, :], act[frame * 128 : frame * 128 + 256, :], NT)
        taps[frame] = pair[:, 0:128]
        taps[frame + 1] = pair[:, 128:256]
    column = iota((16, 128), 1) % 64

    def across(parts):
        left = jnp.where(column == 0, 0.0, pltpu.roll(parts[0], 1, 1))
        right = jnp.where(column == 63, 0.0, pltpu.roll(parts[2], 127, 1))
        return parts[1] + left + right

    upper = iota((16, 128), 1) < 64
    for frame in range(4):
        total = None
        for delay in range(3):
            part = taps[table[frame * 3 + delay], delay * 144 : delay * 144 + 144, :]
            total = part if total is None else total + part
        step = [
            across([total[(a * 3 + col) * 16 : (a * 3 + col) * 16 + 16] for col in range(3)])
            for a in range(3)
        ]
        from_above = jnp.where(upper, 0.0, pltpu.roll(step[0], 64, 1))
        from_below = jnp.where(upper, pltpu.roll(step[2], 64, 1), 0.0)
        here = slice(frame * 128, frame * 128 + 128)
        own[:, here] = base[:, here] + step[1] + from_above + from_below
        half = slice(frame * 64, frame * 64 + 64)
        above, below = step[2][:, 0:64], step[0][:, 64:128]
        first[:, half] = jnp.where(even, below, above)
        second[:, half] = jnp.where(even, above, below)


def convolve(table, act, folded, base):
    smem = pl.BlockSpec(memory_space=pltpu.SMEM)
    vmem = pl.BlockSpec(memory_space=pltpu.VMEM)
    return pl.pallas_call(
        conv_kernel,
        in_specs=[smem] + [vmem] * 4,
        out_specs=(vmem, vmem, vmem),
        out_shape=(
            jax.ShapeDtypeStruct((16, 512), f32),
            jax.ShapeDtypeStruct((16, 256), f32),
            jax.ShapeDtypeStruct((16, 256), f32),
        ),
        scratch_shapes=[pltpu.VMEM((512, 512), bf16), pltpu.VMEM((6, 432, 128), f32)],
        compiler_params=pltpu.CompilerParams(vmem_limit_bytes=10 * MIB),
        cost_estimate=pl.CostEstimate(flops=4 * 10**8, bytes_accessed=2 * 10**6, transcendentals=0),
        name="convolve",
    )(table, act, *folded, base)


def finish_kernel(own, first, second, out):
    even = lax.axis_index("head") % 2 == 0
    lane = iota((16, 128), 1)
    row = iota((128, 128), 0)
    pos = iota((128, 128), 1)
    own_half = (pos % 64) // 32 == row // 64
    own_cell = (pos // 64) * 2 + pos % 2 == row % 4
    keep = own_half & own_cell
    repeat = (iota((128, 16), 0) % 64 // 4 == iota((128, 16), 1)).astype(bf16)
    pick = ((lane % 32) // 2 == iota((16, 128), 0)).astype(bf16)
    for frame in range(4):
        half = slice(frame * 64, frame * 64 + 64)
        one, two = first[:, half], second[:, half]
        edge = jnp.concatenate([jnp.where(even, two, one), jnp.where(even, one, two)], axis=1)
        latent = ((own[:, frame * 128 : frame * 128 + 128] + edge) * latent_scale).astype(bf16)
        wide = jnp.where(keep, dot(repeat, latent), 0.0).astype(bf16)
        piece = dot(pick, wide, NT).astype(bf16)
        for peer in range(out.shape[0]):
            out[peer, frame] = piece


def finish(own, first, second, copies):
    vmem = pl.BlockSpec(memory_space=pltpu.VMEM)
    return pl.pallas_call(
        finish_kernel,
        in_specs=[vmem, vmem, vmem],
        out_specs=vmem,
        out_shape=jax.ShapeDtypeStruct((copies, 4, 16, 128), bf16),
        compiler_params=pltpu.CompilerParams(vmem_limit_bytes=6 * MIB),
        cost_estimate=pl.CostEstimate(flops=10**7, bytes_accessed=10**6, transcendentals=0),
        name="finish",
    )(own, first, second)


def route_kernel(table, frames, mine, other):
    core = lax.axis_index("seq") % 2
    for out, owner in ((mine, core), (other, 1 - core)):
        for slot in range(4):
            frame = table[12 + owner * 4 + slot]
            here = (frame // 4) % 2 == core
            piece = frames[frame // 8, frame % 4]
            out[slot] = jnp.where(here, piece, jnp.zeros_like(piece))


def route(table, frames):
    smem = pl.BlockSpec(memory_space=pltpu.SMEM)
    vmem = pl.BlockSpec(memory_space=pltpu.VMEM)
    shape = jax.ShapeDtypeStruct((4, 16, 128), bf16)
    return pl.pallas_call(
        route_kernel,
        in_specs=[smem, vmem],
        out_specs=(vmem, vmem),
        out_shape=(shape, shape),
        compiler_params=pltpu.CompilerParams(vmem_limit_bytes=4 * MIB),
        cost_estimate=pl.CostEstimate(flops=1, bytes_accessed=10**6, transcendentals=0),
        name="route",
    )(table, frames)


def scale_kernel(member, modulation, embed, bias, left, gram, gvec):
    width = embed.shape[1]
    chunk = 512
    mean = jnp.sum(embed[...].astype(f32), axis=1, keepdims=True) / width
    bias_mean = jnp.sum(bias[...], axis=1, keepdims=True) / width
    whole = jnp.zeros((80, 80), f32)
    for at in range(0, width, chunk):
        here = slice(at, at + chunk)
        centred = embed[:, here].astype(f32) - mean
        cbias = bias[:, here] - bias_mean
        scale = 1.0 + dot(member[...], modulation[:, width + at : width + at + chunk])
        shift = dot(member[...], modulation[:, here])
        first, second = scale[0:1], scale[1:2]
        high, low = split2(centred * first)
        left[0:64, here] = high
        left[64:128, here] = low
        high, low = split2(centred * second)
        left[128:192, here] = high
        left[192:256, here] = low
        high, low = split2(jnp.concatenate([cbias * first, cbias * second], axis=0))
        left[256:272, here] = jnp.concatenate(
            [high.astype(f32), low.astype(f32), shift[0:2], jnp.zeros((10, chunk), f32)], axis=0
        ).astype(bf16)
        full = jnp.concatenate([centred, cbias, jnp.zeros((15, chunk), f32)], axis=0)
        high, low = split2(full)
        whole = whole + (dot(high, high, NT) + dot(high, low, NT) + dot(low, high, NT))
    whole = whole * (1.0 / width)
    square = whole[0:64, 0:64]
    blank = jnp.zeros((64, 64), f32)
    block = jnp.concatenate(
        [jnp.concatenate([square, blank], axis=1), jnp.concatenate([blank, square], axis=1)], axis=0
    )
    top = block.astype(bf16)
    rest = block - top.astype(f32)
    mid = rest.astype(bf16)
    gram[0] = top
    gram[1] = mid
    gram[2] = (rest - mid.astype(f32)).astype(bf16)
    cross = 2.0 * whole[64:65, 0:64]
    const = jnp.broadcast_to(whole[64:65, 64:65], (1, 128))
    gvec[...] = jnp.concatenate(
        [jnp.concatenate([cross, cross], axis=1), const, jnp.zeros((6, 128), f32)], axis=0
    )


def scale_embedding(member, modulation, embed_weight, embed_bias):
    width = embed_weight.shape[1]
    vmem = pl.BlockSpec(memory_space=pltpu.VMEM)
    return pl.pallas_call(
        scale_kernel,
        in_specs=[vmem] * 4,
        out_specs=[vmem] * 3,
        out_shape=[
            jax.ShapeDtypeStruct((272, width), bf16),
            jax.ShapeDtypeStruct((3, 128, 128), bf16),
            jax.ShapeDtypeStruct((8, 128), f32),
        ],
        compiler_params=pltpu.CompilerParams(vmem_limit_bytes=8 * MIB),
        cost_estimate=pl.CostEstimate(flops=10**8, bytes_accessed=3 * 10**6, transcendentals=0),
        name="scale_embedding",
    )(member, modulation, embed_weight, embed_bias.reshape(1, -1))


def mix_kernel(left, qkv_w, qkv_b, mix, rows, held, sems):
    parts, depth = held.shape[0], held.shape[1]
    copies = [
        pltpu.make_async_copy(qkv_w.at[pl.ds(k * depth, depth)], held.at[k], sems.at[k])
        for k in range(parts)
    ]
    for copy in copies:
        copy.start()
    product = None
    for k in range(parts):
        copies[k].wait()
        term = dot(left[:, k * depth : k * depth + depth], held[k])
        product = term if product is None else product + term
    for clip in range(2):
        at = clip * 128
        high, low = split2(product[at : at + 64] + product[at + 64 : at + 128])
        mix[clip] = jnp.concatenate([high, low], axis=0)
    tail = product[256:272]
    rows[...] = jnp.concatenate(
        [tail[0:2] + tail[2:4], tail[4:6] + qkv_b[...], jnp.zeros((4, 768), f32)], axis=0
    )


def mix_weights(left, qkv_weight, qkv_bias):
    vmem = pl.BlockSpec(memory_space=pltpu.VMEM)
    return pl.pallas_call(
        mix_kernel,
        in_specs=[vmem, pl.BlockSpec(memory_space=pl.ANY), vmem],
        out_specs=[vmem, vmem],
        out_shape=[
            jax.ShapeDtypeStruct((2, 128, 768), bf16),
            jax.ShapeDtypeStruct((8, 768), f32),
        ],
        scratch_shapes=[pltpu.VMEM((4, 768, 768), bf16), pltpu.SemaphoreType.DMA((4,))],
        compiler_params=pltpu.CompilerParams(vmem_limit_bytes=56 * MIB),
        cost_estimate=pl.CostEstimate(flops=13 * 10**8, bytes_accessed=6 * 10**6, transcendentals=0),
        name="mix_weights",
    )(left, qkv_weight, qkv_bias.reshape(1, -1))


def project(clip, begin, end, tokens, mix, rows, gram, gvec, q_gain, k_gain, parts):
    factor = math.log2(math.e) / math.sqrt(128)
    gain = q_gain[...] * k_gain[...] * factor
    own = jnp.concatenate([tokens[:, frame].reshape(128, 128) for frame in range(begin, end)], axis=0)
    spread = dot(own, gram[0]) + dot(own, gram[1]) + dot(own, gram[2])
    terms = (spread + gvec[0:1, :]) * own.astype(f32)
    low_lane = iota(own.shape, 1) < 64
    for half in range(2):
        mine = jnp.where(low_lane == (half == 0), terms, 0.0)
        variance = jnp.sum(mine, axis=1, keepdims=True) + gvec[1:2, 0:1]
        scale = lax.rsqrt(jnp.maximum(variance, 0.0) + norm_eps)
        feats = own[:, half * 64 : half * 64 + 64]
        twice = jnp.concatenate([feats, feats], axis=1)
        qkv = scale * (dot(twice, mix[clip]) + rows[clip : clip + 1, :]) + rows[clip + 2 : clip + 3, :]
        for head in range(2):
            at = head * 384
            for kind in range(3):
                part = qkv[:, at + kind * 128 : at + kind * 128 + 128]
                if kind < 2:
                    part = part * lax.rsqrt(jnp.mean(part * part, axis=1, keepdims=True) + norm_eps)
                if kind == 0:
                    part = part * gain
                part = part.astype(bf16)
                for frame in range(begin, end):
                    place = frame * 256 + half * 128
                    parts[kind, head, place : place + 128, :] = part[
                        (frame - begin) * 128 : (frame - begin) * 128 + 128
                    ]


def attend_kernel(
    table, tokens, mix, rows, gram, gvec, q_gain, k_gain, out, parts
):
    lead = table[20]
    shared = (tokens, mix, rows, gram, gvec, q_gain, k_gain, parts)

    def group(begin, end):
        for head in range(2):
            key = parts[1, head, begin * 256 : end * 256, :]
            value = parts[2, head, begin * 256 : end * 256, :]
            wide = jnp.concatenate([value, jnp.ones_like(value)], axis=1)
            for frame in range(begin, end):
                score = dot(parts[0, head, frame * 256 : frame * 256 + 256, :], key, NT)
                top = jnp.max(score, axis=1, keepdims=True)
                expo = jnp.exp2(score - top)
                both = dot(expo.astype(bf16), wide)
                result = (both[:, 0:128] / both[:, 128:256]).astype(bf16)
                lanes = slice(head * 128, head * 128 + 128)
                for half in range(2):
                    for band in range(8):
                        at = (half * 8 + band) * 16
                        out[7 - band, frame, half, :, lanes] = result[at : at + 16]

    for first in (1, 2, 3):

        @pl.when(lead == first)
        def _(first=first):
            project(0, 0, first, *shared)
            project(1, first, 4, *shared)
            group(0, first)
            group(first, 4)


def attend(table, tokens, mix, rows, gram, gvec, q_gain, k_gain):
    smem = pl.BlockSpec(memory_space=pltpu.SMEM)
    vmem = pl.BlockSpec(memory_space=pltpu.VMEM)
    return pl.pallas_call(
        attend_kernel,
        in_specs=[smem] + [vmem] * 7,
        out_specs=vmem,
        out_shape=jax.ShapeDtypeStruct((8, 4, 2, 16, 256), bf16),
        scratch_shapes=[pltpu.VMEM((3, 2, 1024, 128), bf16)],
        compiler_params=pltpu.CompilerParams(vmem_limit_bytes=14 * MIB),
        cost_estimate=pl.CostEstimate(flops=10**9, bytes_accessed=3 * 10**6, transcendentals=1300000),
        name="attend",
    )(table, tokens, mix, rows, gram, gvec, q_gain, k_gain)


def neighbour(value, axis, step):
    count = lax.axis_size(axis)
    pairs = [(i, i + step) for i in range(count) if 0 <= i + step < count]
    return lax.ppermute(value, axis, pairs)


def swap(value, axis, mask):
    return lax.ppermute(value, axis, [(i, i ^ mask) for i in range(lax.axis_size(axis))])


def swap_pairs(value, axis, begin):
    pairs = [(i, i + 1) for i in range(begin, lax.axis_size(axis) - 1, 2)]
    return lax.ppermute(value, axis, pairs + [(b, a) for a, b in pairs])


def swap3(value, axis, unit):
    return [value] + [swap(value, axis, unit * step) for step in (3, 2, 1)][::-1]


def per_device(
    video_feat,
    clip_frames,
    clip_offset,
    conv_weight,
    conv_bias,
    latent_weight,
    latent_bias,
    embed_weight,
    embed_bias,
    modulation,
    qkv_weight,
    qkv_bias,
    q_gain,
    k_gain,
):
    seqs, heads = lax.axis_size("seq"), lax.axis_size("head")
    seq = lax.axis_index("seq")
    frames = video_feat.shape[0]
    latent_rows = latent_weight.T

    weight = conv_weight.transpose(0, 1, 2, 4, 3).reshape(27, conv_weight.shape[4], -1)
    parts = lax.all_to_all(
        fold_tap(weight, latent_rows, heads), "head", 0, 0, axis_index_groups=[list(range(heads))[::-1]]
    )
    prev = neighbour(video_feat[2:], "seq", 1)
    tap = jnp.sum(parts.astype(f32), axis=0).astype(bf16)

    count = clip_frames.shape[0]
    numbers = jnp.arange(count, dtype=jnp.int32)
    starts = jnp.sum(jnp.where(numbers[None, :] < numbers[:, None], clip_frames[None, :], 0), axis=1)
    ids = seq * frames + jnp.arange(frames, dtype=jnp.int32)
    first = jnp.max(jnp.where(starts[None, :] <= ids[:, None], starts[None, :], 0), axis=1)
    slot = seq // 2 * 2 * frames + jnp.arange(2 * frames, dtype=jnp.int32)
    inside = (clip_offset[None, :] <= slot[:, None]) & (
        slot[:, None] < (clip_offset + clip_frames)[None, :]
    )
    origin = jnp.sum(jnp.where(inside, (starts - clip_offset)[None, :] + slot[:, None], 0), axis=1)
    origin = jnp.clip(origin, 0, seqs * frames - 1)
    delays = jnp.arange(3, dtype=jnp.int32)
    source = jnp.maximum(ids[:, None] - 2 + delays[None, :], first[:, None]) - seq * frames + 2
    source = jnp.clip(source, 0, frames + 1).reshape(-1)
    leading = clip_offset == seq * frames
    lead = jnp.sum(jnp.where(leading, clip_frames, 0)).reshape(1)
    table = jnp.concatenate([source, origin, lead])
    trailing = (clip_offset > seq * frames) & (clip_offset < (seq + 1) * frames)
    member = jnp.concatenate(
        [leading[None], trailing[None], jnp.zeros((6, count), jnp.bool_)], axis=0
    ).astype(bf16)

    left, gram, gvec = scale_embedding(member, modulation, embed_weight, embed_bias)

    tap, table = lax.optimization_barrier((tap, table))
    chips = seqs // 2
    cores = [[2 * chip + core for chip in range(chips)] for core in range(2)]
    over_chips = lambda value: lax.all_to_all(value, "seq", 0, 0, axis_index_groups=cores)
    same = over_chips(jnp.broadcast_to(tap[None], (chips,) + tap.shape))
    mix, rows = mix_weights(left, qkv_weight, qkv_bias)
    mixed = mix, rows, gram, gvec
    same, mixed = lax.optimization_barrier((same, mixed))
    folded = same, swap(same, "seq", 1)
    act, base = prepare(video_feat, prev, latent_rows, conv_bias, latent_bias)

    own, first, second = convolve(table, act, folded, base)
    first = swap_pairs(first, "head", 0)
    second = swap_pairs(second, "head", 1)
    pieces = finish(own, first, second, chips)
    frames_all = over_chips(pieces)
    mine, other = route(table, frames_all)
    slots = mine + swap(other, "seq", 1)
    tokens = lax.all_to_all(
        jnp.broadcast_to(slots[None], (heads,) + slots.shape), "head", 0, 0, axis_index_groups=[list(range(heads))[::-1]]
    )
    gains = q_gain.reshape(1, -1), k_gain.reshape(1, -1)
    out = attend(table, tokens, *mixed, *gains)
    return out.reshape(heads * frames * 32, 256)


def solution(mesh):
    placed = (
        P("seq", "head", None, None),
        P(),
        P(),
        P(None, None, None, None, "head"),
        P(),
        P(),
        P(),
        P(),
        P(),
        P(),
        P(None, "head"),
        P("head"),
        P(),
        P(),
    )
    return jax.shard_map(
        per_device, mesh=mesh, in_specs=placed, out_specs=P("seq", "head"), check_vma=False
    )
```
